32 devices in a mesh: parts: 2 (over y), seq: 16 (over z, x, core).
Axes of the slice: x: 2, y: 2, z: 4, core: 2. Of those that a mesh axis runs over, the one named last changes fastest.
Arguments:
- queries: bfloat16 [32, 8192], P(('parts', 'seq')), parts along dimension 0, may hold values from -140 to 140
- new_keys: bfloat16 [32, 1024], P(('parts', 'seq')), parts along dimension 0, may hold values from -7 to 7
- new_values: bfloat16 [32, 1024], P(('parts', 'seq')), parts along dimension 0, may hold values from -6 to 6
- doc_keys: bfloat16 [32768, 1024], P(('parts', 'seq')), parts along dimension 0, may hold values from -6 to 6
- doc_values: bfloat16 [32768, 1024], P(('parts', 'seq')), parts along dimension 0, may hold values from -6 to 6
- suffix_keys: bfloat16 [32768, 1024], P(('parts', 'seq')), parts along dimension 0, may hold values from -6 to 6
- suffix_values: bfloat16 [32768, 1024], P(('parts', 'seq')), parts along dimension 0, may hold values from -6 to 6
- keep_lists: int32 [32, 32], P(('parts', 'seq')), parts along dimension 0, may hold values from 0 to 127, as said below
- suffix_lengths: int32 [16], P('parts'), parts along dimension 0, may hold values from 1 to 2048
Outputs:
- attended: bfloat16 [32, 8192], P(('parts', 'seq')), parts along dimension 0
The draws below stay inside these ranges and needn't reach their ends.
There are 2 independent parts, one for each index of `parts`. The reference program is written for one: setup_inputs(seed, part) draws one part's arguments, and reference() takes and returns one part's arrays. A program takes and returns all parts, laid end to end along the dimension named above; each array names one. Nothing has to cross between parts.
Inputs may be any that keep to these rules, and one draw needn't show every extreme that they name: Row r's list (rows 2r and 2r+1 of keep_lists) names 64 different blocks of 0 to 127.
All inputs are finite; a program needn't handle non-finite values.
Results may differ from the reference program's by a relative error of at most 0.007.
Values may be sent and summed in bfloat16 or wider, within the bound.
A program may use at most 128 MiB of HBM per device.

```python
import jax
import jax.numpy as jnp
from jax import lax

HEADS = 64
KVH = 8
HD = 128
BLOCK = 128
DOC_DEV = 1024
SUF_DEV = 1024
ROWS = 8
QTOK = 16
SUFFIX = 2048
L_DOC = 16384
CORPUS_TILES = 128
KEEP = 64
N_SEQ = 16


def common_new(key):
    fresh = jnp.clip(jax.random.normal(jax.random.fold_in(key, 11), (QTOK, KVH * HD), jnp.float32), -6.0, 6.0)
    return fresh


def draw_new_keys(key, part):
    return common_new(key).astype(jnp.bfloat16)


def draw_queries(key, part):
    fresh = common_new(key)
    drawn_sample = 3.0 * jnp.clip(jax.random.normal(jax.random.fold_in(key, 13), (QTOK, HEADS * HD), jnp.float32), -4.0, 4.0)
    own_part = jnp.repeat(fresh.reshape(QTOK, KVH, 1, HD), HEADS // KVH, axis=2).reshape(QTOK, HEADS * HD)
    result = drawn_sample + 1.3 * own_part
    return result.astype(jnp.bfloat16)


def draw_doc_values(key, part):
    fluctuation = jnp.clip(jax.random.normal(jax.random.fold_in(key, 31), (L_DOC, KVH * HD), jnp.float32), -4.0, 4.0)
    column_offset = jnp.clip(jax.random.normal(jax.random.fold_in(key, 32), (KVH * HD,), jnp.float32), -2.0, 2.0)
    return (fluctuation + column_offset[None, :]).astype(jnp.bfloat16)


def draw_keep_lists(key, part):
    shard_mass = jax.random.randint(jax.random.fold_in(key, 21), (N_SEQ,), 0, 3) * 32768
    holding_shard = jnp.arange(CORPUS_TILES, dtype=jnp.int32) // (CORPUS_TILES // N_SEQ)
    extra_credit = shard_mass[holding_shard]
    stochastic_jitter = jax.random.randint(jax.random.fold_in(key, 22), (ROWS, CORPUS_TILES), 0, 65536)
    sorted_position = (stochastic_jitter + extra_credit[None, :]) * CORPUS_TILES + jnp.arange(CORPUS_TILES, dtype=jnp.int32)[None, :]
    _, selected_entries = lax.top_k(sorted_position, KEEP)
    return selected_entries.astype(jnp.int32).reshape(QTOK, KEEP // 2)


def set_ends(drawn, own_key, smallest, high):
    index_at = [jax.random.randint(jax.random.fold_in(own_key, axis), (), 0, length) for axis, length in enumerate(drawn.shape)]
    longest = drawn.shape.index(max(drawn.shape))
    beside = index_at[:longest] + [(index_at[longest] + 1) % drawn.shape[longest]] + index_at[longest + 1:]
    return drawn.at[tuple(index_at)].set(smallest).at[tuple(beside)].set(high)


def level_of(own_key, shape, shards, low, largest):
    level = 1.0
    for dim, shards_of in shards:
        steps = jax.random.uniform(jax.random.fold_in(jax.random.fold_in(own_key, 6), dim), (shards_of,), jnp.float32, low / len(shards), largest / len(shards))
        level = level * jnp.repeat(jnp.exp(steps), shape[dim] // shards_of).reshape((-1,) + (1,) * (len(shape) - 1 - dim))
    return level


def normal_values(stream_key, shape, spread, reach, cuts=(), held_as=jnp.bfloat16):
    loudness = level_of(stream_key, shape, cuts, -0.22, 0.18) if cuts else 1.0
    values = jax.random.normal(stream_key, shape, jnp.float32) * spread * loudness
    return jnp.minimum(jnp.maximum(values, -reach), reach).astype(held_as)


def setup_inputs(seed: int = 0, part: int = 0) -> dict:
    key_of = jax.random.split(jax.random.key(seed), 10)
    part_splits = jax.random.split(jax.random.fold_in(key_of[9], part), 10)
    queries = draw_queries(jax.random.fold_in(jax.random.fold_in(key_of[9], part), 71), part)
    new_keys = draw_new_keys(jax.random.fold_in(jax.random.fold_in(key_of[9], part), 71), part)
    new_values = normal_values(part_splits[2], (QTOK, KVH * HD), 1.0, 6.0, ((0, 16),))
    doc_keys = normal_values(part_splits[3], (L_DOC, KVH * HD), 1.0, 6.0, ((0, 16),))
    doc_values = draw_doc_values(jax.random.fold_in(jax.random.fold_in(key_of[9], part), 71), part)
    suffix_keys = normal_values(part_splits[5], (ROWS * SUFFIX, KVH * HD), 1.0, 6.0, ((0, 16),))
    suffix_values = normal_values(part_splits[6], (ROWS * SUFFIX, KVH * HD), 1.0, 6.0, ((0, 16),))
    keep_lists = draw_keep_lists(jax.random.fold_in(jax.random.fold_in(key_of[9], part), 71), part)
    suffix_lengths = set_ends(jax.random.randint(part_splits[8], (ROWS,), 1, SUFFIX + 1), jax.random.fold_in(part_splits[8], 1), 1, SUFFIX).astype(jnp.int32)
    return {"queries": queries, "new_keys": new_keys, "new_values": new_values, "doc_keys": doc_keys, "doc_values": doc_values, "suffix_keys": suffix_keys, "suffix_values": suffix_values, "keep_lists": keep_lists, "suffix_lengths": suffix_lengths}


NEG_BIG = -1e30


def merge_terms(first, second):
    ceiling = jnp.maximum(first[0], second[0])
    left_scale = jnp.exp(first[0] - ceiling)
    right_scale = jnp.exp(second[0] - ceiling)
    return (ceiling, left_scale * first[1] + right_scale * second[1],
            left_scale[..., None] * first[2] + right_scale[..., None] * second[2])


def block_parts(scores, live_keys, value_rows):
    masked = jnp.where(live_keys, scores, NEG_BIG)
    block_max = jnp.max(masked, axis=-1)
    weights = jnp.where(live_keys, jnp.exp(scores - block_max[..., None]), 0.0)
    block_sum = jnp.sum(weights, axis=-1)
    rounded = lax.optimization_barrier(weights.astype(jnp.bfloat16)).astype(jnp.float32)
    block_out = jnp.einsum("tkgbj,bjkd->tkgbd", rounded, value_rows)
    return block_max, block_sum, block_out


def collapse(parts):
    block_max, block_sum, block_out = parts
    global_maximum = jnp.max(block_max, axis=-1)
    factor = jnp.exp(block_max - global_maximum[..., None])
    return (global_maximum, jnp.sum(factor * block_sum, axis=-1), jnp.sum(factor[..., None] * block_out, axis=-2))


def reference(queries, new_keys, new_values, doc_keys, doc_values, suffix_keys, suffix_values, keep_lists, suffix_lengths):
    groups = HEADS // KVH
    factor_scale = HD ** -0.5
    keep_rows = keep_lists.reshape(ROWS, KEEP)
    group_len = 8 if KEEP % 8 == 0 else 1
    doc_kblocks = doc_keys.reshape(CORPUS_TILES, BLOCK, KVH, HD)
    doc_vblocks = doc_values.reshape(CORPUS_TILES, BLOCK, KVH, HD)
    half_blocks = SUF_DEV // BLOCK
    span_blocks = DOC_DEV // BLOCK

    def one_row(row_id):
        q_rows = lax.dynamic_slice_in_dim(queries, (2 * row_id).astype(jnp.int32), 2, 0)
        q_rows = q_rows.astype(jnp.float32).reshape(2, KVH, groups, HD)

        def visit_group(block_ids):
            keys_now = doc_kblocks[block_ids].astype(jnp.float32)
            values_now = doc_vblocks[block_ids].astype(jnp.float32)
            scores = jnp.einsum("tkgd,bjkd->tkgbj", q_rows, keys_now) * factor_scale
            return block_parts(scores, True, values_now)

        ids = keep_rows[row_id]
        b_max, b_sum, b_out = lax.map(visit_group, ids.reshape(KEEP // group_len, group_len))
        b_max = jnp.moveaxis(b_max, 0, 3).reshape(2, KVH, groups, KEEP)
        b_sum = jnp.moveaxis(b_sum, 0, 3).reshape(2, KVH, groups, KEEP)
        b_out = jnp.moveaxis(b_out, 0, 3).reshape(2, KVH, groups, KEEP, HD)
        span_of = ids // span_blocks
        member = span_of[:, None] == jnp.arange(N_SEQ, dtype=jnp.int32)[None, :]
        span_max = jnp.max(jnp.where(member, b_max[..., None], NEG_BIG), axis=-2)
        back_max = jnp.max(jnp.where(member, span_max[..., None, :], NEG_BIG), axis=-1)
        factor = jnp.exp(b_max - back_max)
        onehot = member.astype(jnp.float32)
        span_sum = jnp.einsum("tkgb,bs->tkgs", factor * b_sum, onehot, precision=lax.Precision.HIGHEST)
        span_out = jnp.einsum("tkgbd,bs->tkgsd", factor[..., None] * b_out, onehot, precision=lax.Precision.HIGHEST)

        offset = (row_id * SUFFIX).astype(jnp.int32)
        keys_new = lax.dynamic_slice_in_dim(new_keys, (2 * row_id).astype(jnp.int32), 2, 0)
        keys_new = keys_new.astype(jnp.float32).reshape(2, KVH, HD)
        values_new = lax.dynamic_slice_in_dim(new_values, (2 * row_id).astype(jnp.int32), 2, 0)
        values_new = values_new.astype(jnp.float32).reshape(2, KVH, HD)
        own_scores = jnp.einsum("tkgd,ukd->tkgu", q_rows, keys_new) * factor_scale
        visible = (jnp.arange(2)[None, :] <= jnp.arange(2)[:, None])[:, None, None, :]
        for half in range(2):
            start = offset + half * SUF_DEV
            keys_suf = lax.dynamic_slice_in_dim(suffix_keys, start, SUF_DEV, 0).astype(jnp.float32)
            keys_suf = keys_suf.reshape(half_blocks, BLOCK, KVH, HD)
            values_suf = lax.dynamic_slice_in_dim(suffix_values, start, SUF_DEV, 0).astype(jnp.float32)
            values_suf = values_suf.reshape(half_blocks, BLOCK, KVH, HD)
            scores = jnp.einsum("tkgd,bjkd->tkgbj", q_rows, keys_suf) * factor_scale
            position = half * SUF_DEV + jnp.arange(SUF_DEV, dtype=jnp.int32).reshape(half_blocks, BLOCK)
            live_keys = position < suffix_lengths[row_id]
            suffix_part = collapse(block_parts(scores, live_keys, values_suf))
            seen = visible[..., half]
            own_part = (jnp.where(seen, own_scores[..., half], NEG_BIG),
                        jnp.where(seen, 1.0, 0.0) * jnp.ones_like(own_scores[..., half]),
                        jnp.where(seen[..., None], values_new[None, half][:, :, None, :], 0.0) * jnp.ones_like(q_rows))
            span_id = (2 * row_id + half).astype(jnp.int32)
            doc_part = (lax.dynamic_index_in_dim(span_max, span_id, 3, False),
                        lax.dynamic_index_in_dim(span_sum, span_id, 3, False),
                        lax.dynamic_index_in_dim(span_out, span_id, 3, False))
            joined = merge_terms(merge_terms(doc_part, suffix_part), own_part)
            span_max = lax.dynamic_update_index_in_dim(span_max, joined[0], span_id, 3)
            span_sum = lax.dynamic_update_index_in_dim(span_sum, joined[1], span_id, 3)
            span_out = lax.dynamic_update_index_in_dim(span_out, joined[2], span_id, 3)
        units = span_out / jnp.maximum(span_sum, 1.0)[..., None]
        units = lax.optimization_barrier(units.astype(jnp.bfloat16)).astype(jnp.float32)
        ceiling = jnp.max(span_max, axis=-1)
        weight = jnp.exp(span_max - ceiling[..., None]) * span_sum
        total_out = jnp.sum(weight[..., None] * units, axis=-2)
        total_sum = jnp.sum(weight, axis=-1)
        return (total_out / total_sum[..., None]).reshape(2, HEADS * HD)

    result = lax.map(one_row, jnp.arange(ROWS, dtype=jnp.int32))
    return result.reshape(QTOK, HEADS * HD).astype(jnp.bfloat16)
```

```python
import functools
import math

import jax
import jax.numpy as jnp
from jax import lax
from jax.experimental import pallas as pl
from jax.experimental.pallas import tpu as pltpu
from jax.sharding import PartitionSpec as P

HD = 128
BLOCK = 128
LANES = 128
TOKENS = 16

DEAD = -1e30
FLOOR = -1e29
MESH = pl.DeviceIdType.MESH
COEF = HD ** (-0.5) * math.log2(math.e)
NT = (((1,), (1,)), ((), ()))
NN = (((1,), (0,)), ((), ()))


def softmax_terms(scores, bias, values):
    rows, group, keys = scores.shape
    masked = scores + bias
    top = jnp.maximum(jnp.max(masked, axis=-1, keepdims=True), FLOOR)
    weights = jnp.exp2((masked - top) * COEF)
    total = jnp.sum(weights, axis=-1, keepdims=True)
    out = lax.dot_general(
        weights.reshape(rows * group, keys).astype(jnp.bfloat16),
        values,
        NN,
        preferred_element_type=jnp.float32,
    )
    return top, total, out.reshape(rows, group, HD)


def kernel(
    n, kvh, group,
    len_ref, q_ref, nk_ref, nv_ref, keep_ref, dk_hbm, dv_hbm, sk_hbm, sv_hbm,
    out_ref,
    dk, dv, sk, sv, q_rows, q_all, lists, bias_ref, units, stats, suf_units, suf_stats,
    in_units, in_stats,
    load_sem, q_send, q_recv, l_send, l_recv, u_send, u_recv, s_send, s_recv, p_send, p_recv,
):
    part = lax.axis_index("parts")
    me = lax.axis_index("seq")
    row = me // 2
    parity = me % 2
    partner = me + 1 - 2 * parity
    heads = kvh * group
    keys = dk.shape[0]
    blocks = keys // BLOCK

    def peer_of(i):
        return lax.rem(2 * row + i + 1, n)

    loads = []
    for index, (source, target) in enumerate(((sk_hbm, sk), (sv_hbm, sv), (dk_hbm, dk), (dv_hbm, dv))):
        load = pltpu.make_async_copy(source, target, load_sem.at[index])
        load.start()
        loads.append(load)

    barrier = pltpu.get_barrier_semaphore()
    pl.semaphore_signal(barrier, inc=1, device_id=(part, partner), device_id_type=MESH)

    def greet(i, carry):
        pl.semaphore_signal(barrier, inc=1, device_id=(part, peer_of(i)), device_id_type=MESH)
        return carry

    lax.fori_loop(1, n - 1, greet, 0)

    for h in range(heads):
        q_rows[h : h + 1, :] = q_ref[0:1, h * HD : (h + 1) * HD].astype(jnp.float32)
    q_all[me] = q_rows[...].astype(jnp.bfloat16)
    kept = keep_ref.shape[1]
    width = lists.shape[2]
    ids = keep_ref[...]
    blank = jnp.full((1, kept), -1, jnp.int32)
    pieces = [jnp.where(parity == 0, ids, blank), jnp.where(parity == 1, ids, blank)]
    if width > 2 * kept:
        pieces.append(jnp.full((1, width - 2 * kept), -1, jnp.int32))
    lists[me] = jnp.broadcast_to(jnp.concatenate(pieces, axis=1), (8, width))

    pl.semaphore_wait(barrier, n - 1)

    def q_copy(peer, slot):
        return pltpu.make_async_remote_copy(
            src_ref=q_all.at[slot], dst_ref=q_all.at[slot],
            send_sem=q_send.at[peer], recv_sem=q_recv.at[slot],
            device_id=(part, peer), device_id_type=MESH,
        )

    def l_copy(peer, slot):
        return pltpu.make_async_remote_copy(
            src_ref=lists.at[slot], dst_ref=lists.at[slot],
            send_sem=l_send.at[peer], recv_sem=l_recv.at[slot],
            device_id=(part, peer), device_id_type=MESH,
        )

    def u_copy(peer, slot, target):
        return pltpu.make_async_remote_copy(
            src_ref=units.at[slot], dst_ref=in_units.at[target],
            send_sem=u_send.at[peer], recv_sem=u_recv.at[target],
            device_id=(part, peer), device_id_type=MESH,
        )

    def s_copy(peer, slot, target):
        return pltpu.make_async_remote_copy(
            src_ref=stats.at[slot], dst_ref=in_stats.at[target],
            send_sem=s_send.at[peer], recv_sem=s_recv.at[target],
            device_id=(part, peer), device_id_type=MESH,
        )

    q_copy(partner, me).start()
    l_copy(partner, me).start()

    def share(i, carry):
        q_copy(peer_of(i), me).start()
        l_copy(peer_of(i), me).start()
        return carry

    lax.fori_loop(1, n - 1, share, 0)

    lane = lax.broadcasted_iota(jnp.int32, (1, group, LANES), 2)
    position = parity * keys + lax.broadcasted_iota(jnp.int32, (1, group, keys), 2)
    suf_bias = jnp.where(position < len_ref[row], 0.0, DEAD)
    token = lax.broadcasted_iota(jnp.int32, (2, group, 1), 0)
    visible = token >= parity
    q_copy(partner, partner).wait_recv()
    loads[0].wait()
    loads[1].wait()
    stat = jnp.zeros((2, group, LANES), jnp.float32)
    for pair in range(kvh // 2):
        q_pair = q_all[pl.ds(2 * row, 2), 2 * group * pair : 2 * group * (pair + 1), :].astype(jnp.float32)
        made = []
        for half in range(2):
            h = 2 * pair + half
            cols = slice(h * HD, (h + 1) * HD)
            q_head = q_pair[:, half * group : (half + 1) * group, :]
            scores = lax.dot_general(
                q_head.reshape(2 * group, HD).astype(jnp.bfloat16), sk[:, cols], NT,
                preferred_element_type=jnp.float32,
            ).reshape(2, group, keys)
            top, total, out = softmax_terms(scores, suf_bias, sv[:, cols])
            new_key = nk_ref[0:1, cols].astype(jnp.float32).reshape(1, 1, HD)
            new_value = nv_ref[0:1, cols].astype(jnp.float32).reshape(1, 1, HD)
            own = jnp.where(visible, jnp.sum(q_head * new_key, axis=-1, keepdims=True), DEAD)
            joint = jnp.maximum(top, own)
            old_scale = jnp.exp2((top - joint) * COEF)
            own_scale = jnp.exp2((own - joint) * COEF)
            total = old_scale * total + own_scale
            out = old_scale * out + own_scale * new_value
            made.append(out / jnp.maximum(total, 1.0))
            stat = jnp.where(lane == h, joint, stat)
            stat = jnp.where(lane == kvh + h, total, stat)
        suf_units[:, 2 * group * pair : 2 * group * (pair + 1), :] = jnp.concatenate(made, axis=1).astype(jnp.bfloat16)
    suf_stats[...] = stat
    in_units[n] = suf_units[parity]
    in_stats[n] = suf_stats[parity]
    suffix_copies = [
        pltpu.make_async_remote_copy(
            src_ref=source.at[1 - parity], dst_ref=target.at[n + 1],
            send_sem=p_send.at[index], recv_sem=p_recv.at[index],
            device_id=(part, partner), device_id_type=MESH,
        )
        for index, (source, target) in enumerate(((suf_units, in_units), (suf_stats, in_stats)))
    ]
    for copy in suffix_copies:
        copy.start()

    l_copy(partner, partner).wait_recv()

    def arrive(i, carry):
        q_copy(peer_of(i), peer_of(i)).wait_recv()
        l_copy(peer_of(i), peer_of(i)).wait_recv()
        return carry

    lax.fori_loop(1, n - 1, arrive, 0)
    loads[2].wait()
    loads[3].wait()
    chunk = min(n, TOKENS)

    def span(start):
        both = lists[pl.ds(start, chunk)].reshape(chunk // 2, 2, 8, width)
        both = jnp.maximum(both[:, 0], both[:, 1])
        for b in range(blocks):
            hit = jnp.max(jnp.where(both == me * blocks + b, 0.0, DEAD), axis=-1, keepdims=True)
            bias_ref[:, :, b * BLOCK : (b + 1) * BLOCK] = jnp.broadcast_to(hit, (chunk // 2, 8, BLOCK))
        stat = jnp.zeros((chunk, group, LANES), jnp.float32)
        for pair in range(kvh // 2):
            q_pair = q_all[pl.ds(start, chunk), 2 * group * pair : 2 * group * (pair + 1), :].astype(jnp.float32)
            made = []
            for half in range(2):
                h = 2 * pair + half
                cols = slice(h * HD, (h + 1) * HD)
                q_head = q_pair[:, half * group : (half + 1) * group, :]
                scores = lax.dot_general(
                    q_head.reshape(chunk * group, HD).astype(jnp.bfloat16), dk[:, cols], NT,
                    preferred_element_type=jnp.float32,
                ).reshape(chunk, group, keys)
                bias = jnp.broadcast_to(
                    bias_ref[...][:, None], (chunk // 2, 2, group, keys)
                ).reshape(chunk, group, keys)
                top, total, out = softmax_terms(scores, bias, dv[:, cols])
                made.append(out * (1.0 / jnp.maximum(total, 1.0)))
                stat = jnp.where(lane == h, top, stat)
                stat = jnp.where(lane == kvh + h, total, stat)
            units[pl.ds(start, chunk), 2 * group * pair : 2 * group * (pair + 1), :] = jnp.concatenate(made, axis=1).astype(jnp.bfloat16)
        stats[pl.ds(start, chunk)] = stat

    if n > chunk:
        def step(c, carry):
            span(c * chunk)
            return carry

        lax.fori_loop(0, n // chunk, step, 0)
    else:
        span(0)

    def deliver(i, carry):
        s_copy(peer_of(i), peer_of(i), me).start()
        u_copy(peer_of(i), peer_of(i), me).start()
        return carry

    lax.fori_loop(1, n - 1, deliver, 0)
    s_copy(partner, partner, me).start()
    u_copy(partner, partner, me).start()
    in_units[me] = units[me]
    in_stats[me] = stats[me]
    q_copy(partner, me).wait_send()
    l_copy(partner, me).wait_send()

    def q_sent(i, carry):
        q_copy(peer_of(i), me).wait_send()
        l_copy(peer_of(i), me).wait_send()
        return carry

    lax.fori_loop(1, n - 1, q_sent, 0)
    for copy in suffix_copies:
        copy.wait()
    s_copy(partner, partner, partner).wait_recv()
    u_copy(partner, partner, partner).wait_recv()

    def collect(i, carry):
        s_copy(peer_of(i), peer_of(i), peer_of(i)).wait_recv()
        u_copy(peer_of(i), peer_of(i), peer_of(i)).wait_recv()
        return carry

    lax.fori_loop(1, n - 1, collect, 0)

    tops = in_stats[...]
    ceiling = jnp.max(tops, axis=0, keepdims=True)
    spread = jnp.exp2((tops - ceiling) * COEF)
    sums = pltpu.roll(tops.reshape((n + 2) * group, LANES), LANES - kvh, 1).reshape(n + 2, group, LANES)
    weight = spread * sums
    weight = weight / jnp.sum(weight, axis=0, keepdims=True)
    for pair in range(kvh // 2):
        parts = in_units[:, 2 * group * pair : 2 * group * (pair + 1), :].astype(jnp.float32)
        ends = []
        for half in range(2):
            h = 2 * pair + half
            ends.append(jnp.sum(weight[:, :, h : h + 1] * parts[:, half * group : (half + 1) * group, :], axis=0))
        out_ref[2 * group * pair : 2 * group * (pair + 1), :] = jnp.concatenate(ends, axis=0).astype(out_ref.dtype)

    s_copy(partner, partner, me).wait_send()
    u_copy(partner, partner, me).wait_send()

    def u_sent(i, carry):
        s_copy(peer_of(i), peer_of(i), me).wait_send()
        u_copy(peer_of(i), peer_of(i), me).wait_send()
        return carry

    lax.fori_loop(1, n - 1, u_sent, 0)


def per_device(n, queries, new_keys, new_values, doc_keys, doc_values, suffix_keys, suffix_values, keep_lists, suffix_lengths):
    heads = queries.shape[1] // HD
    kvh = new_keys.shape[1] // HD
    group = heads // kvh
    width = -(-2 * keep_lists.shape[1] // LANES) * LANES
    keys, columns = doc_keys.shape
    vmem = pl.BlockSpec(memory_space=pltpu.VMEM)
    smem = pl.BlockSpec(memory_space=pltpu.SMEM)
    anywhere = pl.BlockSpec(memory_space=pl.ANY)
    dma = pltpu.SemaphoreType.DMA
    out = pl.pallas_call(
        functools.partial(kernel, n, kvh, group),
        out_shape=jax.ShapeDtypeStruct((heads, HD), jnp.bfloat16),
        in_specs=[smem, vmem, vmem, vmem, vmem, anywhere, anywhere, anywhere, anywhere],
        out_specs=vmem,
        scratch_shapes=[
            pltpu.VMEM((keys, columns), jnp.bfloat16),
            pltpu.VMEM((keys, columns), jnp.bfloat16),
            pltpu.VMEM(suffix_keys.shape, jnp.bfloat16),
            pltpu.VMEM(suffix_keys.shape, jnp.bfloat16),
            pltpu.VMEM((heads, HD), jnp.float32),
            pltpu.VMEM((n, heads, HD), jnp.bfloat16),
            pltpu.VMEM((n, 8, width), jnp.int32),
            pltpu.VMEM((min(n, TOKENS) // 2, 8, keys), jnp.float32),
            pltpu.VMEM((n, heads, HD), jnp.bfloat16),
            pltpu.VMEM((n, group, LANES), jnp.float32),
            pltpu.VMEM((2, heads, HD), jnp.bfloat16),
            pltpu.VMEM((2, group, LANES), jnp.float32),
            pltpu.VMEM((n + 2, heads, HD), jnp.bfloat16),
            pltpu.VMEM((n + 2, group, LANES), jnp.float32),
            dma((4,)),
            dma((n,)), dma((n,)), dma((n,)), dma((n,)),
            dma((n,)), dma((n,)), dma((n,)), dma((n,)),
            dma((2,)), dma((2,)),
        ],
        compiler_params=pltpu.CompilerParams(
            collective_id=0, has_side_effects=True, vmem_limit_bytes=48 * 1024 * 1024
        ),
    )(suffix_lengths, queries, new_keys, new_values, keep_lists, doc_keys, doc_values, suffix_keys, suffix_values)
    return out.reshape(1, heads * HD)


def solution(mesh):
    rows = P(("parts", "seq"), None)
    return jax.shard_map(
        functools.partial(per_device, mesh.shape["seq"]),
        mesh=mesh,
        in_specs=(rows,) * 8 + (P("parts"),),
        out_specs=rows,
        check_vma=False,
    )
```

```python
import functools
import math

import jax
import jax.numpy as jnp
from jax import lax
from jax.experimental import pallas as pl
from jax.experimental.pallas import tpu as pltpu
from jax.sharding import PartitionSpec as P

HD = 128
BLOCK = 128
LANES = 128
TOKENS = 16

DEAD = -1e30
FLOOR = -1e29
MESH = pl.DeviceIdType.MESH
COEF = HD ** (-0.5) * math.log2(math.e)
NT = (((1,), (1,)), ((), ()))
NN = (((1,), (0,)), ((), ()))


def softmax_terms(scores, bias, values):
    rows, group, keys = scores.shape
    masked = scores + bias
    top = jnp.maximum(jnp.max(masked, axis=-1, keepdims=True), FLOOR)
    weights = jnp.exp2((masked - top) * COEF)
    total = jnp.sum(weights, axis=-1, keepdims=True)
    out = lax.dot_general(
        weights.reshape(rows * group, keys).astype(jnp.bfloat16),
        values,
        NN,
        preferred_element_type=jnp.float32,
    )
    return top, total, out.reshape(rows, group, HD)


def kernel(
    n, kvh, group,
    len_hbm, q_hbm, nk_hbm, nv_hbm, keep_hbm, dk_hbm, dv_hbm, sk_hbm, sv_hbm,
    out_ref,
    len_ref, q_ref, nk_ref, nv_ref, keep_ref,
    dk, dv, sk, sv, q_rows, q_all, lists, bias_ref, units, stats, suf_units, suf_stats,
    in_units, in_stats,
    load_sem, q_send, q_recv, l_send, l_recv, u_send, u_recv, s_send, s_recv, p_send, p_recv,
):
    part = lax.axis_index("parts")
    me = lax.axis_index("seq")
    row = me // 2
    parity = me % 2
    partner = me + 1 - 2 * parity
    heads = kvh * group
    keys = dk.shape[0]
    blocks = keys // BLOCK

    def peer_of(i):
        return lax.rem(2 * row + i + 1, n)

    loads = []
    pairs = (
        (q_hbm, q_ref), (keep_hbm, keep_ref), (len_hbm, len_ref), (nk_hbm, nk_ref), (nv_hbm, nv_ref),
        (sk_hbm, sk), (sv_hbm, sv), (dk_hbm, dk), (dv_hbm, dv),
    )
    for index, (source, target) in enumerate(pairs):
        load = pltpu.make_async_copy(source, target, load_sem.at[index])
        load.start()
        loads.append(load)

    barrier = pltpu.get_barrier_semaphore()
    pl.semaphore_signal(barrier, inc=1, device_id=(part, partner), device_id_type=MESH)

    def greet(i, carry):
        pl.semaphore_signal(barrier, inc=1, device_id=(part, peer_of(i)), device_id_type=MESH)
        return carry

    lax.fori_loop(1, n - 1, greet, 0)

    loads[0].wait()
    for h in range(heads):
        q_rows[h : h + 1, :] = q_ref[0:1, h * HD : (h + 1) * HD].astype(jnp.float32)
    q_all[me] = q_rows[...].astype(jnp.bfloat16)
    kept = keep_ref.shape[1]
    width = lists.shape[2]
    loads[1].wait()
    ids = keep_ref[...]
    blank = jnp.full((1, kept), -1, jnp.int32)
    pieces = [jnp.where(parity == 0, ids, blank), jnp.where(parity == 1, ids, blank)]
    if width > 2 * kept:
        pieces.append(jnp.full((1, width - 2 * kept), -1, jnp.int32))
    lists[me] = jnp.broadcast_to(jnp.concatenate(pieces, axis=1), (8, width))

    pl.semaphore_wait(barrier, n - 1)

    def q_copy(peer, slot):
        return pltpu.make_async_remote_copy(
            src_ref=q_all.at[slot], dst_ref=q_all.at[slot],
            send_sem=q_send.at[peer], recv_sem=q_recv.at[slot],
            device_id=(part, peer), device_id_type=MESH,
        )

    def l_copy(peer, slot):
        return pltpu.make_async_remote_copy(
            src_ref=lists.at[slot], dst_ref=lists.at[slot],
            send_sem=l_send.at[peer], recv_sem=l_recv.at[slot],
            device_id=(part, peer), device_id_type=MESH,
        )

    def u_copy(peer, slot, target):
        return pltpu.make_async_remote_copy(
            src_ref=units.at[slot], dst_ref=in_units.at[target],
            send_sem=u_send.at[peer], recv_sem=u_recv.at[target],
            device_id=(part, peer), device_id_type=MESH,
        )

    def s_copy(peer, slot, target):
        return pltpu.make_async_remote_copy(
            src_ref=stats.at[slot], dst_ref=in_stats.at[target],
            send_sem=s_send.at[peer], recv_sem=s_recv.at[target],
            device_id=(part, peer), device_id_type=MESH,
        )

    q_copy(partner, me).start()
    l_copy(partner, me).start()

    def share(i, carry):
        q_copy(peer_of(i), me).start()
        l_copy(peer_of(i), me).start()
        return carry

    lax.fori_loop(1, n - 1, share, 0)

    loads[2].wait()
    loads[3].wait()
    loads[4].wait()
    lane = lax.broadcasted_iota(jnp.int32, (1, group, LANES), 2)
    position = parity * keys + lax.broadcasted_iota(jnp.int32, (1, group, keys), 2)
    suf_bias = jnp.where(position < len_ref[row], 0.0, DEAD)
    token = lax.broadcasted_iota(jnp.int32, (2, group, 1), 0)
    visible = token >= parity
    q_copy(partner, partner).wait_recv()
    loads[5].wait()
    loads[6].wait()
    stat = jnp.zeros((2, group, LANES), jnp.float32)
    for pair in range(kvh // 2):
        q_pair = q_all[pl.ds(2 * row, 2), 2 * group * pair : 2 * group * (pair + 1), :].astype(jnp.float32)
        made = []
        for half in range(2):
            h = 2 * pair + half
            cols = slice(h * HD, (h + 1) * HD)
            q_head = q_pair[:, half * group : (half + 1) * group, :]
            scores = lax.dot_general(
                q_head.reshape(2 * group, HD).astype(jnp.bfloat16), sk[:, cols], NT,
                preferred_element_type=jnp.float32,
            ).reshape(2, group, keys)
            top, total, out = softmax_terms(scores, suf_bias, sv[:, cols])
            new_key = nk_ref[0:1, cols].astype(jnp.float32).reshape(1, 1, HD)
            new_value = nv_ref[0:1, cols].astype(jnp.float32).reshape(1, 1, HD)
            own = jnp.where(visible, jnp.sum(q_head * new_key, axis=-1, keepdims=True), DEAD)
            joint = jnp.maximum(top, own)
            old_scale = jnp.exp2((top - joint) * COEF)
            own_scale = jnp.exp2((own - joint) * COEF)
            total = old_scale * total + own_scale
            out = old_scale * out + own_scale * new_value
            made.append(out / jnp.maximum(total, 1.0))
            stat = jnp.where(lane == h, joint, stat)
            stat = jnp.where(lane == kvh + h, total, stat)
        suf_units[:, 2 * group * pair : 2 * group * (pair + 1), :] = jnp.concatenate(made, axis=1).astype(jnp.bfloat16)
    suf_stats[...] = stat
    in_units[n] = suf_units[parity]
    in_stats[n] = suf_stats[parity]
    suffix_copies = [
        pltpu.make_async_remote_copy(
            src_ref=source.at[1 - parity], dst_ref=target.at[n + 1],
            send_sem=p_send.at[index], recv_sem=p_recv.at[index],
            device_id=(part, partner), device_id_type=MESH,
        )
        for index, (source, target) in enumerate(((suf_units, in_units), (suf_stats, in_stats)))
    ]
    for copy in suffix_copies:
        copy.start()

    l_copy(partner, partner).wait_recv()

    def arrive(i, carry):
        q_copy(peer_of(i), peer_of(i)).wait_recv()
        l_copy(peer_of(i), peer_of(i)).wait_recv()
        return carry

    lax.fori_loop(1, n - 1, arrive, 0)
    loads[7].wait()
    loads[8].wait()
    chunk = min(n, TOKENS)

    def span(start):
        both = lists[pl.ds(start, chunk)].reshape(chunk // 2, 2, 8, width)
        both = jnp.maximum(both[:, 0], both[:, 1])
        for b in range(blocks):
            hit = jnp.max(jnp.where(both == me * blocks + b, 0.0, DEAD), axis=-1, keepdims=True)
            bias_ref[:, :, b * BLOCK : (b + 1) * BLOCK] = jnp.broadcast_to(hit, (chunk // 2, 8, BLOCK))
        stat = jnp.zeros((chunk, group, LANES), jnp.float32)
        for pair in range(kvh // 2):
            q_pair = q_all[pl.ds(start, chunk), 2 * group * pair : 2 * group * (pair + 1), :].astype(jnp.float32)
            made = []
            for half in range(2):
                h = 2 * pair + half
                cols = slice(h * HD, (h + 1) * HD)
                q_head = q_pair[:, half * group : (half + 1) * group, :]
                scores = lax.dot_general(
                    q_head.reshape(chunk * group, HD).astype(jnp.bfloat16), dk[:, cols], NT,
                    preferred_element_type=jnp.float32,
                ).reshape(chunk, group, keys)
                bias = jnp.broadcast_to(
                    bias_ref[...][:, None], (chunk // 2, 2, group, keys)
                ).reshape(chunk, group, keys)
                top, total, out = softmax_terms(scores, bias, dv[:, cols])
                made.append(out * (1.0 / jnp.maximum(total, 1.0)))
                stat = jnp.where(lane == h, top, stat)
                stat = jnp.where(lane == kvh + h, total, stat)
            units[pl.ds(start, chunk), 2 * group * pair : 2 * group * (pair + 1), :] = jnp.concatenate(made, axis=1).astype(jnp.bfloat16)
        stats[pl.ds(start, chunk)] = stat

    if n > chunk:
        def step(c, carry):
            span(c * chunk)
            return carry

        lax.fori_loop(0, n // chunk, step, 0)
    else:
        span(0)

    def deliver(i, carry):
        s_copy(peer_of(i), peer_of(i), me).start()
        u_copy(peer_of(i), peer_of(i), me).start()
        return carry

    lax.fori_loop(1, n - 1, deliver, 0)
    s_copy(partner, partner, me).start()
    u_copy(partner, partner, me).start()
    in_units[me] = units[me]
    in_stats[me] = stats[me]
    q_copy(partner, me).wait_send()
    l_copy(partner, me).wait_send()

    def q_sent(i, carry):
        q_copy(peer_of(i), me).wait_send()
        l_copy(peer_of(i), me).wait_send()
        return carry

    lax.fori_loop(1, n - 1, q_sent, 0)
    for copy in suffix_copies:
        copy.wait()
    s_copy(partner, partner, partner).wait_recv()
    u_copy(partner, partner, partner).wait_recv()

    def collect(i, carry):
        s_copy(peer_of(i), peer_of(i), peer_of(i)).wait_recv()
        u_copy(peer_of(i), peer_of(i), peer_of(i)).wait_recv()
        return carry

    lax.fori_loop(1, n - 1, collect, 0)

    tops = in_stats[...]
    ceiling = jnp.max(tops, axis=0, keepdims=True)
    spread = jnp.exp2((tops - ceiling) * COEF)
    sums = pltpu.roll(tops.reshape((n + 2) * group, LANES), LANES - kvh, 1).reshape(n + 2, group, LANES)
    weight = spread * sums
    weight = weight / jnp.sum(weight, axis=0, keepdims=True)
    for pair in range(kvh // 2):
        parts = in_units[:, 2 * group * pair : 2 * group * (pair + 1), :].astype(jnp.float32)
        ends = []
        for half in range(2):
            h = 2 * pair + half
            ends.append(jnp.sum(weight[:, :, h : h + 1] * parts[:, half * group : (half + 1) * group, :], axis=0))
        out_ref[2 * group * pair : 2 * group * (pair + 1), :] = jnp.concatenate(ends, axis=0).astype(out_ref.dtype)

    s_copy(partner, partner, me).wait_send()
    u_copy(partner, partner, me).wait_send()

    def u_sent(i, carry):
        s_copy(peer_of(i), peer_of(i), me).wait_send()
        u_copy(peer_of(i), peer_of(i), me).wait_send()
        return carry

    lax.fori_loop(1, n - 1, u_sent, 0)


def per_device(n, queries, new_keys, new_values, doc_keys, doc_values, suffix_keys, suffix_values, keep_lists, suffix_lengths):
    heads = queries.shape[1] // HD
    kvh = new_keys.shape[1] // HD
    group = heads // kvh
    width = -(-2 * keep_lists.shape[1] // LANES) * LANES
    keys, columns = doc_keys.shape
    hbm = pl.BlockSpec(memory_space=pltpu.HBM)
    dma = pltpu.SemaphoreType.DMA
    out = pl.pallas_call(
        functools.partial(kernel, n, kvh, group),
        out_shape=jax.ShapeDtypeStruct((heads, HD), jnp.bfloat16),
        in_specs=[hbm] * 9,
        out_specs=pl.BlockSpec(memory_space=pltpu.VMEM),
        scratch_shapes=[
            pltpu.SMEM(suffix_lengths.shape, jnp.int32),
            pltpu.VMEM(queries.shape, jnp.bfloat16),
            pltpu.VMEM(new_keys.shape, jnp.bfloat16),
            pltpu.VMEM(new_values.shape, jnp.bfloat16),
            pltpu.VMEM(keep_lists.shape, jnp.int32),
            pltpu.VMEM((keys, columns), jnp.bfloat16),
            pltpu.VMEM((keys, columns), jnp.bfloat16),
            pltpu.VMEM(suffix_keys.shape, jnp.bfloat16),
            pltpu.VMEM(suffix_keys.shape, jnp.bfloat16),
            pltpu.VMEM((heads, HD), jnp.float32),
            pltpu.VMEM((n, heads, HD), jnp.bfloat16),
            pltpu.VMEM((n, 8, width), jnp.int32),
            pltpu.VMEM((min(n, TOKENS) // 2, 8, keys), jnp.float32),
            pltpu.VMEM((n, heads, HD), jnp.bfloat16),
            pltpu.VMEM((n, group, LANES), jnp.float32),
            pltpu.VMEM((2, heads, HD), jnp.bfloat16),
            pltpu.VMEM((2, group, LANES), jnp.float32),
            pltpu.VMEM((n + 2, heads, HD), jnp.bfloat16),
            pltpu.VMEM((n + 2, group, LANES), jnp.float32),
            dma((9,)),
            dma((n,)), dma((n,)), dma((n,)), dma((n,)),
            dma((n,)), dma((n,)), dma((n,)), dma((n,)),
            dma((2,)), dma((2,)),
        ],
        compiler_params=pltpu.CompilerParams(
            collective_id=0, has_side_effects=True, vmem_limit_bytes=65000 * 1024
        ),
    )(suffix_lengths, queries, new_keys, new_values, keep_lists, doc_keys, doc_values, suffix_keys, suffix_values)
    return out.reshape(1, heads * HD)


def solution(mesh):
    rows = P(("parts", "seq"), None)
    return jax.shard_map(
        functools.partial(per_device, mesh.shape["seq"]),
        mesh=mesh,
        in_specs=(rows,) * 8 + (P("parts"),),
        out_specs=rows,
        check_vma=False,
    )
```

```python
import functools
import math

import jax
import jax.numpy as jnp
from jax import lax
from jax.experimental import pallas as pl
from jax.experimental.pallas import tpu as pltpu
from jax.sharding import PartitionSpec as P

HD = 128
BLOCK = 128
LANES = 128
TOKENS = 16

DEAD = -1e30
FLOOR = -1e29
MESH = pl.DeviceIdType.MESH
COEF = HD ** (-0.5) * math.log2(math.e)
NT = (((1,), (1,)), ((), ()))
NN = (((1,), (0,)), ((), ()))


def softmax_terms(scores, bias, values):
    rows, group, keys = scores.shape
    masked = scores + bias
    top = jnp.maximum(jnp.max(masked, axis=-1, keepdims=True), FLOOR)
    weights = jnp.exp2((masked - top) * COEF)
    total = jnp.sum(weights, axis=-1, keepdims=True)
    out = lax.dot_general(
        weights.reshape(rows * group, keys).astype(jnp.bfloat16),
        values,
        NN,
        preferred_element_type=jnp.float32,
    )
    return top, total, out.reshape(rows, group, HD)


def kernel(
    n, kvh, group,
    len_hbm, q_hbm, nk_hbm, nv_hbm, keep_hbm, dk_hbm, dv_hbm, sk_hbm, sv_hbm,
    out_ref,
    len_ref, q_ref, nk_ref, nv_ref, keep_ref,
    dk, dv, sk, sv, q_rows, q_all, lists, bias_ref, units, stats, mate_units, mate_stats, merged, merged_stats, suf_units, suf_stats,
    in_units, in_stats,
    load_sem, q_send, q_recv, l_send, l_recv, m_send, m_recv, u_send, u_recv, s_send, s_recv, p_send, p_recv,
):
    part = lax.axis_index("parts")
    me = lax.axis_index("seq")
    row = me // 2
    parity = me % 2
    partner = me + 1 - 2 * parity
    chips = n // 2
    heads = kvh * group
    keys = dk.shape[0]
    blocks = keys // BLOCK

    def peer_of(i):
        return lax.rem(me + 2 * i, n)

    loads = []
    pairs = (
        (q_hbm, q_ref), (keep_hbm, keep_ref), (len_hbm, len_ref), (nk_hbm, nk_ref), (nv_hbm, nv_ref),
        (sk_hbm, sk), (sv_hbm, sv), (dk_hbm, dk), (dv_hbm, dv),
    )
    for index, (source, target) in enumerate(pairs):
        load = pltpu.make_async_copy(source, target, load_sem.at[index])
        load.start()
        loads.append(load)

    barrier = pltpu.get_barrier_semaphore()
    pl.semaphore_signal(barrier, inc=1, device_id=(part, partner), device_id_type=MESH)

    def greet(i, carry):
        pl.semaphore_signal(barrier, inc=1, device_id=(part, peer_of(i)), device_id_type=MESH)
        return carry

    lax.fori_loop(1, chips, greet, 0)

    loads[0].wait()
    for h in range(heads):
        q_rows[h : h + 1, :] = q_ref[0:1, h * HD : (h + 1) * HD].astype(jnp.float32)
    q_all[me] = q_rows[...].astype(jnp.bfloat16)
    kept = keep_ref.shape[1]
    width = lists.shape[2]
    loads[1].wait()
    ids = keep_ref[...]
    blank = jnp.full((1, kept), -1, jnp.int32)
    pieces = [jnp.where(parity == 0, ids, blank), jnp.where(parity == 1, ids, blank)]
    if width > 2 * kept:
        pieces.append(jnp.full((1, width - 2 * kept), -1, jnp.int32))
    lists[me] = jnp.concatenate(pieces, axis=1)

    pl.semaphore_wait(barrier, chips)

    def q_copy(device, slot, send):
        return pltpu.make_async_remote_copy(
            src_ref=q_all.at[slot], dst_ref=q_all.at[slot],
            send_sem=q_send.at[send], recv_sem=q_recv.at[slot],
            device_id=(part, device), device_id_type=MESH,
        )

    def l_copy(device, slot, send):
        return pltpu.make_async_remote_copy(
            src_ref=lists.at[slot], dst_ref=lists.at[slot],
            send_sem=l_send.at[send], recv_sem=l_recv.at[slot],
            device_id=(part, device), device_id_type=MESH,
        )

    def mate_copy(pair):
        rows = slice(2 * group * pair, 2 * group * (pair + 1))
        return pltpu.make_async_remote_copy(
            src_ref=units.at[1 - parity, :, rows, :], dst_ref=mate_units.at[:, rows, :],
            send_sem=m_send.at[pair], recv_sem=m_recv.at[pair],
            device_id=(part, partner), device_id_type=MESH,
        )

    def mate_stats_copy():
        return pltpu.make_async_remote_copy(
            src_ref=stats.at[1 - parity], dst_ref=mate_stats,
            send_sem=m_send.at[kvh // 2], recv_sem=m_recv.at[kvh // 2],
            device_id=(part, partner), device_id_type=MESH,
        )

    def u_copy(device, target):
        return pltpu.make_async_remote_copy(
            src_ref=merged.at[device // 2], dst_ref=in_units.at[target],
            send_sem=u_send.at[device // 2], recv_sem=u_recv.at[target],
            device_id=(part, device), device_id_type=MESH,
        )

    def s_copy(device, target):
        return pltpu.make_async_remote_copy(
            src_ref=merged_stats.at[device // 2], dst_ref=in_stats.at[target],
            send_sem=s_send.at[device // 2], recv_sem=s_recv.at[target],
            device_id=(part, device), device_id_type=MESH,
        )

    q_copy(partner, me, partner).start()
    l_copy(partner, me, partner).start()

    def share(i, carry):
        q_copy(peer_of(i), me, peer_of(i)).start()
        l_copy(peer_of(i), me, peer_of(i)).start()
        return carry

    lax.fori_loop(1, chips, share, 0)

    loads[2].wait()
    loads[3].wait()
    loads[4].wait()
    lane = lax.broadcasted_iota(jnp.int32, (1, group, LANES), 2)
    position = parity * keys + lax.broadcasted_iota(jnp.int32, (1, group, keys), 2)
    suf_bias = jnp.where(position < len_ref[row], 0.0, DEAD)
    token = lax.broadcasted_iota(jnp.int32, (2, group, 1), 0)
    visible = token >= parity
    q_copy(partner, partner, me).wait_recv()
    loads[5].wait()
    loads[6].wait()
    stat = jnp.zeros((2, group, LANES), jnp.float32)
    for pair in range(kvh // 2):
        q_pair = q_all[pl.ds(2 * row, 2), 2 * group * pair : 2 * group * (pair + 1), :].astype(jnp.float32)
        made = []
        for half in range(2):
            h = 2 * pair + half
            cols = slice(h * HD, (h + 1) * HD)
            q_head = q_pair[:, half * group : (half + 1) * group, :]
            scores = lax.dot_general(
                q_head.reshape(2 * group, HD).astype(jnp.bfloat16), sk[:, cols], NT,
                preferred_element_type=jnp.float32,
            ).reshape(2, group, keys)
            top, total, out = softmax_terms(scores, suf_bias, sv[:, cols])
            new_key = nk_ref[0:1, cols].astype(jnp.float32).reshape(1, 1, HD)
            new_value = nv_ref[0:1, cols].astype(jnp.float32).reshape(1, 1, HD)
            own = jnp.where(visible, jnp.sum(q_head * new_key, axis=-1, keepdims=True), DEAD)
            joint = jnp.maximum(top, own)
            old_scale = jnp.exp2((top - joint) * COEF)
            own_scale = jnp.exp2((own - joint) * COEF)
            total = old_scale * total + own_scale
            out = old_scale * out + own_scale * new_value
            made.append(out / jnp.maximum(total, 1.0))
            stat = jnp.where(lane == h, joint, stat)
            stat = jnp.where(lane == kvh + h, total, stat)
        suf_units[:, 2 * group * pair : 2 * group * (pair + 1), :] = jnp.concatenate(made, axis=1).astype(jnp.bfloat16)
    suf_stats[...] = stat
    in_units[chips] = suf_units[parity]
    in_stats[chips] = suf_stats[parity]
    suffix_copies = [
        pltpu.make_async_remote_copy(
            src_ref=source.at[1 - parity], dst_ref=target.at[chips + 1],
            send_sem=p_send.at[index], recv_sem=p_recv.at[index],
            device_id=(part, partner), device_id_type=MESH,
        )
        for index, (source, target) in enumerate(((suf_units, in_units), (suf_stats, in_stats)))
    ]
    for copy in suffix_copies:
        copy.start()

    l_copy(partner, partner, me).wait_recv()
    flip = 1 - 2 * parity

    def forward(i, carry):
        slot = peer_of(i)
        q_copy(partner, slot, slot + flip).wait_recv()
        q_copy(partner, slot, slot + flip).start()
        l_copy(partner, slot, slot + flip).wait_recv()
        l_copy(partner, slot, slot + flip).start()
        return carry

    lax.fori_loop(1, chips, forward, 0)

    def arrive(i, carry):
        q_copy(partner, peer_of(i) + flip, me).wait_recv()
        l_copy(partner, peer_of(i) + flip, me).wait_recv()
        return carry

    lax.fori_loop(1, chips, arrive, 0)
    loads[7].wait()
    loads[8].wait()
    chunk = min(n, TOKENS)

    def span(start):
        both = lists[pl.ds(start, chunk)].reshape(chunk // 2, 2, 1, width)
        both = jnp.maximum(both[:, 0], both[:, 1])
        for b in range(blocks):
            hit = jnp.max(jnp.where(both == me * blocks + b, 0.0, DEAD), axis=-1, keepdims=True)
            bias_ref[:, :, b * BLOCK : (b + 1) * BLOCK] = jnp.broadcast_to(hit, (chunk // 2, 8, BLOCK))
        stat = jnp.zeros((chunk, group, LANES), jnp.float32)
        for pair in range(kvh // 2):
            q_pair = q_all[pl.ds(start, chunk), 2 * group * pair : 2 * group * (pair + 1), :].astype(jnp.float32)
            made = []
            for half in range(2):
                h = 2 * pair + half
                cols = slice(h * HD, (h + 1) * HD)
                q_head = q_pair[:, half * group : (half + 1) * group, :]
                scores = lax.dot_general(
                    q_head.reshape(chunk * group, HD).astype(jnp.bfloat16), dk[:, cols], NT,
                    preferred_element_type=jnp.float32,
                ).reshape(chunk, group, keys)
                bias = jnp.broadcast_to(
                    bias_ref[...][:, None], (chunk // 2, 2, group, keys)
                ).reshape(chunk, group, keys)
                top, total, out = softmax_terms(scores, bias, dv[:, cols])
                made.append(out * (1.0 / jnp.maximum(total, 1.0)))
                stat = jnp.where(lane == h, top, stat)
                stat = jnp.where(lane == kvh + h, total, stat)
            unit = jnp.concatenate(made, axis=1).astype(jnp.bfloat16).reshape(chunk // 2, 2, 2 * group, HD)
            for side in range(2):
                units[side, pl.ds(start // 2, chunk // 2), 2 * group * pair : 2 * group * (pair + 1), :] = unit[:, side]
            if n == chunk:
                mate_copy(pair).start()
        stat = stat.reshape(chunk // 2, 2, group, LANES)
        for side in range(2):
            stats[side, pl.ds(start // 2, chunk // 2)] = stat[:, side]

    if n > chunk:
        def step(c, carry):
            span(c * chunk)
            return carry

        lax.fori_loop(0, n // chunk, step, 0)
        for pair in range(kvh // 2):
            mate_copy(pair).start()
    else:
        span(0)

    mate_stats_copy().start()

    mate_stats_copy().wait()
    mine, other = stats[parity], mate_stats[...]

    def aligned(values):
        return pltpu.roll(values.reshape(-1, LANES), LANES - kvh, 1).reshape(values.shape)

    joint = jnp.maximum(mine, other)
    mine_part = jnp.exp2((mine - joint) * COEF) * aligned(mine)
    other_part = jnp.exp2((other - joint) * COEF) * aligned(other)
    total = mine_part + other_part
    shares = 1.0 / jnp.maximum(total, 1.0)
    mine_part = mine_part * shares
    other_part = other_part * shares
    shifted = pltpu.roll(total.reshape(-1, LANES), kvh, 1).reshape(total.shape)
    merged_stats[...] = jnp.where(lane < kvh, joint, shifted)
    for pair in range(kvh // 2):
        rows = slice(2 * group * pair, 2 * group * (pair + 1))
        mate_copy(pair).wait()
        first = units[parity, :, rows, :].astype(jnp.float32)
        second = mate_units[:, rows, :].astype(jnp.float32)
        made = []
        for half in range(2):
            h = 2 * pair + half
            part_rows = slice(half * group, (half + 1) * group)
            made.append(
                mine_part[:, :, h : h + 1] * first[:, part_rows, :]
                + other_part[:, :, h : h + 1] * second[:, part_rows, :]
            )
        merged[:, rows, :] = jnp.concatenate(made, axis=1).astype(jnp.bfloat16)

    def deliver(i, carry):
        s_copy(peer_of(i), row).start()
        u_copy(peer_of(i), row).start()
        return carry

    lax.fori_loop(1, chips, deliver, 0)
    in_units[row] = merged[row]
    in_stats[row] = merged_stats[row]
    q_copy(partner, me, partner).wait_send()
    l_copy(partner, me, partner).wait_send()

    def q_sent(i, carry):
        q_copy(peer_of(i), me, peer_of(i)).wait_send()
        l_copy(peer_of(i), me, peer_of(i)).wait_send()
        q_copy(partner, peer_of(i), peer_of(i) + flip).wait_send()
        l_copy(partner, peer_of(i), peer_of(i) + flip).wait_send()
        return carry

    lax.fori_loop(1, chips, q_sent, 0)
    for copy in suffix_copies:
        copy.wait()

    def collect(i, carry):
        s_copy(peer_of(i), peer_of(i) // 2).wait_recv()
        u_copy(peer_of(i), peer_of(i) // 2).wait_recv()
        return carry

    lax.fori_loop(1, chips, collect, 0)

    tops = in_stats[...]
    ceiling = jnp.max(tops, axis=0, keepdims=True)
    spread = jnp.exp2((tops - ceiling) * COEF)
    weight = spread * aligned(tops)
    weight = weight / jnp.sum(weight, axis=0, keepdims=True)
    for pair in range(kvh // 2):
        parts = in_units[:, 2 * group * pair : 2 * group * (pair + 1), :].astype(jnp.float32)
        ends = []
        for half in range(2):
            h = 2 * pair + half
            ends.append(jnp.sum(weight[:, :, h : h + 1] * parts[:, half * group : (half + 1) * group, :], axis=0))
        out_ref[2 * group * pair : 2 * group * (pair + 1), :] = jnp.concatenate(ends, axis=0).astype(out_ref.dtype)

    def u_sent(i, carry):
        s_copy(peer_of(i), row).wait_send()
        u_copy(peer_of(i), row).wait_send()
        return carry

    lax.fori_loop(1, chips, u_sent, 0)


def per_device(n, queries, new_keys, new_values, doc_keys, doc_values, suffix_keys, suffix_values, keep_lists, suffix_lengths):
    heads = queries.shape[1] // HD
    kvh = new_keys.shape[1] // HD
    group = heads // kvh
    width = -(-2 * keep_lists.shape[1] // LANES) * LANES
    keys, columns = doc_keys.shape
    hbm = pl.BlockSpec(memory_space=pltpu.HBM)
    dma = pltpu.SemaphoreType.DMA
    out = pl.pallas_call(
        functools.partial(kernel, n, kvh, group),
        out_shape=jax.ShapeDtypeStruct((heads, HD), jnp.bfloat16),
        in_specs=[hbm] * 9,
        out_specs=pl.BlockSpec(memory_space=pltpu.VMEM),
        scratch_shapes=[
            pltpu.SMEM(suffix_lengths.shape, jnp.int32),
            pltpu.VMEM(queries.shape, jnp.bfloat16),
            pltpu.VMEM(new_keys.shape, jnp.bfloat16),
            pltpu.VMEM(new_values.shape, jnp.bfloat16),
            pltpu.VMEM(keep_lists.shape, jnp.int32),
            pltpu.VMEM((keys, columns), jnp.bfloat16),
            pltpu.VMEM((keys, columns), jnp.bfloat16),
            pltpu.VMEM(suffix_keys.shape, jnp.bfloat16),
            pltpu.VMEM(suffix_keys.shape, jnp.bfloat16),
            pltpu.VMEM((heads, HD), jnp.float32),
            pltpu.VMEM((n, heads, HD), jnp.bfloat16),
            pltpu.VMEM((n, 1, width), jnp.int32),
            pltpu.VMEM((min(n, TOKENS) // 2, 8, keys), jnp.float32),
            pltpu.VMEM((2, n // 2, heads, HD), jnp.bfloat16),
            pltpu.VMEM((2, n // 2, group, LANES), jnp.float32),
            pltpu.VMEM((n // 2, heads, HD), jnp.bfloat16),
            pltpu.VMEM((n // 2, group, LANES), jnp.float32),
            pltpu.VMEM((n // 2, heads, HD), jnp.bfloat16),
            pltpu.VMEM((n // 2, group, LANES), jnp.float32),
            pltpu.VMEM((2, heads, HD), jnp.bfloat16),
            pltpu.VMEM((2, group, LANES), jnp.float32),
            pltpu.VMEM((n // 2 + 2, heads, HD), jnp.bfloat16),
            pltpu.VMEM((n // 2 + 2, group, LANES), jnp.float32),
            dma((9,)),
            dma((n,)), dma((n,)), dma((n,)), dma((n,)),
            dma((kvh // 2 + 1,)), dma((kvh // 2 + 1,)),
            dma((n // 2,)), dma((n // 2,)), dma((n // 2,)), dma((n // 2,)),
            dma((2,)), dma((2,)),
        ],
        compiler_params=pltpu.CompilerParams(
            collective_id=0, has_side_effects=True, vmem_limit_bytes=65000 * 1024
        ),
    )(suffix_lengths, queries, new_keys, new_values, keep_lists, doc_keys, doc_values, suffix_keys, suffix_values)
    return out.reshape(1, heads * HD)


def solution(mesh):
    rows = P(("parts", "seq"), None)
    return jax.shard_map(
        functools.partial(per_device, mesh.shape["seq"]),
        mesh=mesh,
        in_specs=(rows,) * 8 + (P("parts"),),
        out_specs=rows,
        check_vma=False,
    )
```

```python
import functools
import math

import jax
import jax.numpy as jnp
from jax import lax
from jax.experimental import pallas as pl
from jax.experimental.pallas import tpu as pltpu
from jax.sharding import PartitionSpec as P

HD = 128
BLOCK = 128
LANES = 128
TOKENS = 16

DEAD = -1e30
FLOOR = -1e29
MESH = pl.DeviceIdType.MESH
COEF = HD ** (-0.5) * math.log2(math.e)
NT = (((1,), (1,)), ((), ()))
NN = (((1,), (0,)), ((), ()))


def softmax_terms(scores, bias, values):
    rows, group, keys = scores.shape
    masked = scores + bias
    top = jnp.maximum(jnp.max(masked, axis=-1, keepdims=True), FLOOR)
    weights = jnp.exp2((masked - top) * COEF)
    total = jnp.sum(weights, axis=-1, keepdims=True)
    out = lax.dot_general(
        weights.reshape(rows * group, keys).astype(jnp.bfloat16),
        values,
        NN,
        preferred_element_type=jnp.float32,
    )
    return top, total, out.reshape(rows, group, HD)


def kernel(
    n, kvh, group,
    len_hbm, q_hbm, nk_hbm, nv_hbm, keep_hbm, dk_hbm, dv_hbm, sk_hbm, sv_hbm,
    out_ref,
    len_ref, q_ref, nk_ref, nv_ref, keep_ref,
    dk, dv, sk, sv, q_rows, q_all, lists, bias_ref, units, stats, mate_units, mate_stats, merged, merged_stats, suf_units, suf_stats,
    in_units, in_stats,
    load_sem, q_send, q_recv, l_send, l_recv, m_send, m_recv, t_send, t_recv, u_send, u_recv, s_send, s_recv, p_send, p_recv,
):
    part = lax.axis_index("parts")
    me = lax.axis_index("seq")
    row = me // 2
    parity = me % 2
    partner = me + 1 - 2 * parity
    chips = n // 2
    heads = kvh * group
    keys = dk.shape[0]
    blocks = keys // BLOCK

    def peer_of(i):
        return lax.rem(me + 2 * i, n)

    barrier = pltpu.get_barrier_semaphore()
    pl.semaphore_signal(barrier, inc=1, device_id=(part, partner), device_id_type=MESH)

    def greet(i, carry):
        pl.semaphore_signal(barrier, inc=1, device_id=(part, peer_of(i)), device_id_type=MESH)
        return carry

    lax.fori_loop(1, chips, greet, 0)

    loads = []
    pairs = (
        (q_hbm, q_ref), (keep_hbm, keep_ref), (len_hbm, len_ref), (nk_hbm, nk_ref), (nv_hbm, nv_ref),
        (sk_hbm, sk), (sv_hbm, sv), (dk_hbm, dk), (dv_hbm, dv),
    )
    for index, (source, target) in enumerate(pairs):
        load = pltpu.make_async_copy(source, target, load_sem.at[index])
        load.start()
        loads.append(load)

    loads[0].wait()
    for h in range(heads):
        q_rows[h : h + 1, :] = q_ref[0:1, h * HD : (h + 1) * HD].astype(jnp.float32)
    q_all[me] = q_rows[...].astype(jnp.bfloat16)
    kept = keep_ref.shape[1]
    width = lists.shape[2]
    loads[1].wait()
    ids = keep_ref[...]
    blank = jnp.full((1, kept), -1, jnp.int32)
    pieces = [jnp.where(parity == 0, ids, blank), jnp.where(parity == 1, ids, blank)]
    if width > 2 * kept:
        pieces.append(jnp.full((1, width - 2 * kept), -1, jnp.int32))
    lists[me] = jnp.concatenate(pieces, axis=1)

    pl.semaphore_wait(barrier, chips)

    def q_copy(device, slot, send):
        return pltpu.make_async_remote_copy(
            src_ref=q_all.at[slot], dst_ref=q_all.at[slot],
            send_sem=q_send.at[send], recv_sem=q_recv.at[slot],
            device_id=(part, device), device_id_type=MESH,
        )

    def l_copy(device, slot, send):
        return pltpu.make_async_remote_copy(
            src_ref=lists.at[slot], dst_ref=lists.at[slot],
            send_sem=l_send.at[send], recv_sem=l_recv.at[slot],
            device_id=(part, device), device_id_type=MESH,
        )

    def mate_copy(pair):
        rows = slice(2 * group * pair, 2 * group * (pair + 1))
        return pltpu.make_async_remote_copy(
            src_ref=units.at[1 - parity, :, rows, :], dst_ref=mate_units.at[:, rows, :],
            send_sem=m_send.at[pair], recv_sem=m_recv.at[pair],
            device_id=(part, partner), device_id_type=MESH,
        )

    def mate_stats_copy(pair):
        return pltpu.make_async_remote_copy(
            src_ref=stats.at[pair, 1 - parity], dst_ref=mate_stats.at[pair],
            send_sem=t_send.at[pair], recv_sem=t_recv.at[pair],
            device_id=(part, partner), device_id_type=MESH,
        )

    def u_piece(device, target, pair):
        rows = slice(2 * group * pair, 2 * group * (pair + 1))
        return pltpu.make_async_remote_copy(
            src_ref=merged.at[device // 2, rows, :], dst_ref=in_units.at[target, rows, :],
            send_sem=u_send.at[device // 2], recv_sem=u_recv.at[target],
            device_id=(part, device), device_id_type=MESH,
        )

    def u_copy(device, target):
        return pltpu.make_async_remote_copy(
            src_ref=merged.at[device // 2], dst_ref=in_units.at[target],
            send_sem=u_send.at[device // 2], recv_sem=u_recv.at[target],
            device_id=(part, device), device_id_type=MESH,
        )

    def s_copy(device, target):
        return pltpu.make_async_remote_copy(
            src_ref=merged_stats.at[device // 2], dst_ref=in_stats.at[target],
            send_sem=s_send.at[device // 2], recv_sem=s_recv.at[target],
            device_id=(part, device), device_id_type=MESH,
        )

    q_copy(partner, me, partner).start()
    l_copy(partner, me, partner).start()

    def share(i, carry):
        q_copy(peer_of(i), me, peer_of(i)).start()
        l_copy(peer_of(i), me, peer_of(i)).start()
        return carry

    lax.fori_loop(1, chips, share, 0)

    loads[2].wait()
    loads[3].wait()
    loads[4].wait()
    lane = lax.broadcasted_iota(jnp.int32, (1, group, LANES), 2)
    position = parity * keys + lax.broadcasted_iota(jnp.int32, (1, group, keys), 2)
    suf_bias = jnp.where(position < len_ref[row], 0.0, DEAD)
    token = lax.broadcasted_iota(jnp.int32, (2, group, 1), 0)
    visible = token >= parity
    q_copy(partner, partner, me).wait_recv()
    loads[5].wait()
    loads[6].wait()
    stat = jnp.zeros((2, group, LANES), jnp.float32)
    for pair in range(kvh // 2):
        q_pair = q_all[pl.ds(2 * row, 2), 2 * group * pair : 2 * group * (pair + 1), :].astype(jnp.float32)
        made = []
        for half in range(2):
            h = 2 * pair + half
            cols = slice(h * HD, (h + 1) * HD)
            q_head = q_pair[:, half * group : (half + 1) * group, :]
            scores = lax.dot_general(
                q_head.reshape(2 * group, HD).astype(jnp.bfloat16), sk[:, cols], NT,
                preferred_element_type=jnp.float32,
            ).reshape(2, group, keys)
            top, total, out = softmax_terms(scores, suf_bias, sv[:, cols])
            new_key = nk_ref[0:1, cols].astype(jnp.float32).reshape(1, 1, HD)
            new_value = nv_ref[0:1, cols].astype(jnp.float32).reshape(1, 1, HD)
            own = jnp.where(visible, jnp.sum(q_head * new_key, axis=-1, keepdims=True), DEAD)
            joint = jnp.maximum(top, own)
            old_scale = jnp.exp2((top - joint) * COEF)
            own_scale = jnp.exp2((own - joint) * COEF)
            total = old_scale * total + own_scale
            out = old_scale * out + own_scale * new_value
            made.append(out / jnp.maximum(total, 1.0))
            stat = jnp.where(lane == h, joint, stat)
            stat = jnp.where(lane == kvh + h, total, stat)
        suf_units[:, 2 * group * pair : 2 * group * (pair + 1), :] = jnp.concatenate(made, axis=1).astype(jnp.bfloat16)
    suf_stats[...] = stat
    in_units[chips] = suf_units[parity]
    in_stats[chips] = suf_stats[parity]
    suffix_copies = [
        pltpu.make_async_remote_copy(
            src_ref=source.at[1 - parity], dst_ref=target.at[chips + 1],
            send_sem=p_send.at[index], recv_sem=p_recv.at[index],
            device_id=(part, partner), device_id_type=MESH,
        )
        for index, (source, target) in enumerate(((suf_units, in_units), (suf_stats, in_stats)))
    ]
    for copy in suffix_copies:
        copy.start()

    l_copy(partner, partner, me).wait_recv()
    flip = 1 - 2 * parity

    def forward(i, carry):
        slot = peer_of(i)
        q_copy(partner, slot, slot + flip).wait_recv()
        q_copy(partner, slot, slot + flip).start()
        l_copy(partner, slot, slot + flip).wait_recv()
        l_copy(partner, slot, slot + flip).start()
        return carry

    lax.fori_loop(1, chips, forward, 0)

    def arrive(i, carry):
        q_copy(partner, peer_of(i) + flip, me).wait_recv()
        l_copy(partner, peer_of(i) + flip, me).wait_recv()
        return carry

    lax.fori_loop(1, chips, arrive, 0)
    loads[7].wait()
    loads[8].wait()
    chunk = min(n, TOKENS)

    def over_chunks(work):
        if n > chunk:
            def step(c, carry):
                work(c * chunk)
                return carry

            lax.fori_loop(0, n // chunk, step, 0)
        else:
            work(0)

    def mask(start):
        both = lists[pl.ds(start, chunk)].reshape(chunk // 2, 2, 1, width)
        both = jnp.maximum(both[:, 0], both[:, 1])
        for b in range(blocks):
            hit = jnp.max(jnp.where(both == me * blocks + b, 0.0, DEAD), axis=-1, keepdims=True)
            bias_ref[pl.ds(start // 2, chunk // 2), :, b * BLOCK : (b + 1) * BLOCK] = jnp.broadcast_to(hit, (chunk // 2, 8, BLOCK))

    def span(pair, start):
        rows = slice(2 * group * pair, 2 * group * (pair + 1))
        q_pair = q_all[pl.ds(start, chunk), rows, :].astype(jnp.float32)
        stat = jnp.zeros((chunk, group, LANES), jnp.float32)
        made = []
        for half in range(2):
            h = 2 * pair + half
            cols = slice(h * HD, (h + 1) * HD)
            q_head = q_pair[:, half * group : (half + 1) * group, :]
            scores = lax.dot_general(
                q_head.reshape(chunk * group, HD).astype(jnp.bfloat16), dk[:, cols], NT,
                preferred_element_type=jnp.float32,
            ).reshape(chunk, group, keys)
            bias = jnp.broadcast_to(
                bias_ref[pl.ds(start // 2, chunk // 2)][:, None], (chunk // 2, 2, group, keys)
            ).reshape(chunk, group, keys)
            top, total, out = softmax_terms(scores, bias, dv[:, cols])
            made.append(out * (1.0 / jnp.maximum(total, 1.0)))
            stat = jnp.where(lane == h, top, stat)
            stat = jnp.where(lane == kvh + h, total, stat)
        unit = jnp.concatenate(made, axis=1).astype(jnp.bfloat16).reshape(chunk // 2, 2, 2 * group, HD)
        stat = stat.reshape(chunk // 2, 2, group, LANES)
        for side in range(2):
            units[side, pl.ds(start // 2, chunk // 2), rows, :] = unit[:, side]
            stats[pair, side, pl.ds(start // 2, chunk // 2)] = stat[:, side]

    def aligned(values):
        return pltpu.roll(values.reshape(-1, LANES), LANES - kvh, 1).reshape(values.shape)

    def merge(pair):
        rows = slice(2 * group * pair, 2 * group * (pair + 1))
        mate_stats_copy(pair).wait()
        mate_copy(pair).wait()
        mine, other = stats[pair, parity], mate_stats[pair]
        joint = jnp.maximum(mine, other)
        mine_part = jnp.exp2((mine - joint) * COEF) * aligned(mine)
        other_part = jnp.exp2((other - joint) * COEF) * aligned(other)
        total = mine_part + other_part
        shares = 1.0 / jnp.maximum(total, 1.0)
        mine_part = mine_part * shares
        other_part = other_part * shares
        shifted = pltpu.roll(total.reshape(-1, LANES), kvh, 1).reshape(total.shape)
        fresh = jnp.where(lane < kvh, joint, shifted)
        fresh = jnp.where(lax.rem(lane, kvh) // 2 == pair, fresh, 0.0)
        merged_stats[...] = fresh if pair == 0 else merged_stats[...] + fresh
        first = units[parity, :, rows, :].astype(jnp.float32)
        second = mate_units[:, rows, :].astype(jnp.float32)
        made = []
        for half in range(2):
            h = 2 * pair + half
            part_rows = slice(half * group, (half + 1) * group)
            made.append(
                mine_part[:, :, h : h + 1] * first[:, part_rows, :]
                + other_part[:, :, h : h + 1] * second[:, part_rows, :]
            )
        merged[:, rows, :] = jnp.concatenate(made, axis=1).astype(jnp.bfloat16)

        def deliver_piece(i, carry):
            u_piece(peer_of(i), row, pair).start()
            return carry

        lax.fori_loop(1, chips, deliver_piece, 0)

    over_chunks(mask)
    pairs_here = kvh // 2
    for pair in range(pairs_here):
        over_chunks(functools.partial(span, pair))
        mate_stats_copy(pair).start()
        mate_copy(pair).start()
        if pair > 0:
            merge(pair - 1)
    merge(pairs_here - 1)

    def deliver(i, carry):
        s_copy(peer_of(i), row).start()
        return carry

    lax.fori_loop(1, chips, deliver, 0)
    in_units[row] = merged[row]
    in_stats[row] = merged_stats[row]
    q_copy(partner, me, partner).wait_send()
    l_copy(partner, me, partner).wait_send()

    def q_sent(i, carry):
        q_copy(peer_of(i), me, peer_of(i)).wait_send()
        l_copy(peer_of(i), me, peer_of(i)).wait_send()
        q_copy(partner, peer_of(i), peer_of(i) + flip).wait_send()
        l_copy(partner, peer_of(i), peer_of(i) + flip).wait_send()
        return carry

    lax.fori_loop(1, chips, q_sent, 0)
    for copy in suffix_copies:
        copy.wait()

    def collect(i, carry):
        s_copy(peer_of(i), peer_of(i) // 2).wait_recv()
        u_copy(peer_of(i), peer_of(i) // 2).wait_recv()
        return carry

    lax.fori_loop(1, chips, collect, 0)

    tops = in_stats[...]
    ceiling = jnp.max(tops, axis=0, keepdims=True)
    spread = jnp.exp2((tops - ceiling) * COEF)
    weight = spread * aligned(tops)
    weight = weight / jnp.sum(weight, axis=0, keepdims=True)
    for pair in range(kvh // 2):
        parts = in_units[:, 2 * group * pair : 2 * group * (pair + 1), :].astype(jnp.float32)
        ends = []
        for half in range(2):
            h = 2 * pair + half
            ends.append(jnp.sum(weight[:, :, h : h + 1] * parts[:, half * group : (half + 1) * group, :], axis=0))
        out_ref[2 * group * pair : 2 * group * (pair + 1), :] = jnp.concatenate(ends, axis=0).astype(out_ref.dtype)

    def u_sent(i, carry):
        s_copy(peer_of(i), row).wait_send()
        u_copy(peer_of(i), row).wait_send()
        return carry

    lax.fori_loop(1, chips, u_sent, 0)


def per_device(n, queries, new_keys, new_values, doc_keys, doc_values, suffix_keys, suffix_values, keep_lists, suffix_lengths):
    heads = queries.shape[1] // HD
    kvh = new_keys.shape[1] // HD
    group = heads // kvh
    width = -(-2 * keep_lists.shape[1] // LANES) * LANES
    keys, columns = doc_keys.shape
    hbm = pl.BlockSpec(memory_space=pltpu.HBM)
    dma = pltpu.SemaphoreType.DMA
    out = pl.pallas_call(
        functools.partial(kernel, n, kvh, group),
        out_shape=jax.ShapeDtypeStruct((heads, HD), jnp.bfloat16),
        in_specs=[hbm] * 9,
        out_specs=pl.BlockSpec(memory_space=pltpu.VMEM),
        scratch_shapes=[
            pltpu.SMEM(suffix_lengths.shape, jnp.int32),
            pltpu.VMEM(queries.shape, jnp.bfloat16),
            pltpu.VMEM(new_keys.shape, jnp.bfloat16),
            pltpu.VMEM(new_values.shape, jnp.bfloat16),
            pltpu.VMEM(keep_lists.shape, jnp.int32),
            pltpu.VMEM((keys, columns), jnp.bfloat16),
            pltpu.VMEM((keys, columns), jnp.bfloat16),
            pltpu.VMEM(suffix_keys.shape, jnp.bfloat16),
            pltpu.VMEM(suffix_keys.shape, jnp.bfloat16),
            pltpu.VMEM((heads, HD), jnp.float32),
            pltpu.VMEM((n, heads, HD), jnp.bfloat16),
            pltpu.VMEM((n, 1, width), jnp.int32),
            pltpu.VMEM((n // 2, 8, keys), jnp.float32),
            pltpu.VMEM((2, n // 2, heads, HD), jnp.bfloat16),
            pltpu.VMEM((kvh // 2, 2, n // 2, group, LANES), jnp.float32),
            pltpu.VMEM((n // 2, heads, HD), jnp.bfloat16),
            pltpu.VMEM((kvh // 2, n // 2, group, LANES), jnp.float32),
            pltpu.VMEM((n // 2, heads, HD), jnp.bfloat16),
            pltpu.VMEM((n // 2, group, LANES), jnp.float32),
            pltpu.VMEM((2, heads, HD), jnp.bfloat16),
            pltpu.VMEM((2, group, LANES), jnp.float32),
            pltpu.VMEM((n // 2 + 2, heads, HD), jnp.bfloat16),
            pltpu.VMEM((n // 2 + 2, group, LANES), jnp.float32),
            dma((9,)),
            dma((n,)), dma((n,)), dma((n,)), dma((n,)),
            dma((kvh // 2,)), dma((kvh // 2,)), dma((kvh // 2,)), dma((kvh // 2,)),
            dma((n // 2,)), dma((n // 2,)), dma((n // 2,)), dma((n // 2,)),
            dma((2,)), dma((2,)),
        ],
        compiler_params=pltpu.CompilerParams(
            collective_id=0, has_side_effects=True, vmem_limit_bytes=65000 * 1024
        ),
    )(suffix_lengths, queries, new_keys, new_values, keep_lists, doc_keys, doc_values, suffix_keys, suffix_values)
    return out.reshape(1, heads * HD)


def solution(mesh):
    rows = P(("parts", "seq"), None)
    return jax.shard_map(
        functools.partial(per_device, mesh.shape["seq"]),
        mesh=mesh,
        in_specs=(rows,) * 8 + (P("parts"),),
        out_specs=rows,
        check_vma=False,
    )
```

```python
import functools
import math

import jax
import jax.numpy as jnp
from jax import lax
from jax.experimental import pallas as pl
from jax.experimental.pallas import tpu as pltpu
from jax.sharding import PartitionSpec as P

HD = 128
BLOCK = 128
LANES = 128
TOKENS = 16

DEAD = -1e30
FLOOR = -1e29
MESH = pl.DeviceIdType.MESH
COEF = HD ** (-0.5) * math.log2(math.e)
NT = (((1,), (1,)), ((), ()))
NN = (((1,), (0,)), ((), ()))


def softmax_terms(scores, bias, values):
    rows, group, keys = scores.shape
    masked = scores + bias
    top = jnp.maximum(jnp.max(masked, axis=-1, keepdims=True), FLOOR)
    weights = jnp.exp2((masked - top) * COEF)
    total = jnp.sum(weights, axis=-1, keepdims=True)
    out = lax.dot_general(
        weights.reshape(rows * group, keys).astype(jnp.bfloat16),
        values,
        NN,
        preferred_element_type=jnp.float32,
    )
    return top, total, out.reshape(rows, group, HD)


def kernel(
    n, kvh, group,
    len_hbm, q_hbm, nk_hbm, nv_hbm, keep_hbm, dk_hbm, dv_hbm, sk_hbm, sv_hbm,
    out_ref,
    len_ref, q_ref, nk_ref, nv_ref, keep_ref,
    dk, dv, sk, sv, q_rows, q_all, lists, bias_ref, units, stats, mate_units, mate_stats, merged, merged_stats, suf_units, suf_stats,
    in_units, in_stats,
    load_sem, q_send, q_recv, l_send, l_recv, m_send, m_recv, t_send, t_recv, u_send, u_recv, s_send, s_recv, p_send, p_recv,
):
    part = lax.axis_index("parts")
    me = lax.axis_index("seq")
    row = me // 2
    parity = me % 2
    partner = me + 1 - 2 * parity
    chips = n // 2
    heads = kvh * group
    keys = dk.shape[0]
    blocks = keys // BLOCK

    def peer_of(i):
        return lax.rem(me + 2 * i, n)

    def each_chip(work):
        if chips <= TOKENS:
            for i in range(1, chips):
                work(i, 0)
        else:
            lax.fori_loop(1, chips, work, 0)

    barrier = pltpu.get_barrier_semaphore()
    pl.semaphore_signal(barrier, inc=1, device_id=(part, partner), device_id_type=MESH)

    def greet(i, carry):
        pl.semaphore_signal(barrier, inc=1, device_id=(part, peer_of(i)), device_id_type=MESH)
        return carry

    each_chip(greet)

    loads = []
    pairs = (
        (q_hbm, q_ref), (keep_hbm, keep_ref), (len_hbm, len_ref), (nk_hbm, nk_ref), (nv_hbm, nv_ref),
        (sk_hbm, sk), (sv_hbm, sv), (dk_hbm, dk), (dv_hbm, dv),
    )
    for index, (source, target) in enumerate(pairs):
        load = pltpu.make_async_copy(source, target, load_sem.at[index])
        load.start()
        loads.append(load)

    loads[0].wait()
    for h in range(heads):
        q_rows[h : h + 1, :] = q_ref[0:1, h * HD : (h + 1) * HD].astype(jnp.float32)
    q_all[me] = q_rows[...].astype(jnp.bfloat16)
    kept = keep_ref.shape[1]
    width = lists.shape[2]
    loads[1].wait()
    ids = keep_ref[...]
    blank = jnp.full((1, kept), -1, jnp.int32)
    pieces = [jnp.where(parity == 0, ids, blank), jnp.where(parity == 1, ids, blank)]
    if width > 2 * kept:
        pieces.append(jnp.full((1, width - 2 * kept), -1, jnp.int32))
    lists[me] = jnp.concatenate(pieces, axis=1)

    pl.semaphore_wait(barrier, chips)

    def q_copy(device, slot, send):
        return pltpu.make_async_remote_copy(
            src_ref=q_all.at[slot], dst_ref=q_all.at[slot],
            send_sem=q_send.at[send], recv_sem=q_recv.at[slot],
            device_id=(part, device), device_id_type=MESH,
        )

    def l_copy(device, slot, send):
        return pltpu.make_async_remote_copy(
            src_ref=lists.at[slot], dst_ref=lists.at[slot],
            send_sem=l_send.at[send], recv_sem=l_recv.at[slot],
            device_id=(part, device), device_id_type=MESH,
        )

    def mate_copy(pair):
        rows = slice(2 * group * pair, 2 * group * (pair + 1))
        return pltpu.make_async_remote_copy(
            src_ref=units.at[1 - parity, :, rows, :], dst_ref=mate_units.at[:, rows, :],
            send_sem=m_send.at[pair], recv_sem=m_recv.at[pair],
            device_id=(part, partner), device_id_type=MESH,
        )

    def mate_stats_copy(pair):
        return pltpu.make_async_remote_copy(
            src_ref=stats.at[pair, 1 - parity], dst_ref=mate_stats.at[pair],
            send_sem=t_send.at[pair], recv_sem=t_recv.at[pair],
            device_id=(part, partner), device_id_type=MESH,
        )

    def u_piece(device, target, pair):
        rows = slice(2 * group * (pair - 1), 2 * group * (pair + 1))
        return pltpu.make_async_remote_copy(
            src_ref=merged.at[device // 2, rows, :], dst_ref=in_units.at[target, rows, :],
            send_sem=u_send.at[device // 2], recv_sem=u_recv.at[target],
            device_id=(part, device), device_id_type=MESH,
        )

    def u_copy(device, target):
        return pltpu.make_async_remote_copy(
            src_ref=merged.at[device // 2], dst_ref=in_units.at[target],
            send_sem=u_send.at[device // 2], recv_sem=u_recv.at[target],
            device_id=(part, device), device_id_type=MESH,
        )

    def s_copy(device, target):
        return pltpu.make_async_remote_copy(
            src_ref=merged_stats.at[device // 2], dst_ref=in_stats.at[target],
            send_sem=s_send.at[device // 2], recv_sem=s_recv.at[target],
            device_id=(part, device), device_id_type=MESH,
        )

    q_copy(partner, me, partner).start()
    l_copy(partner, me, partner).start()

    def share(i, carry):
        q_copy(peer_of(i), me, peer_of(i)).start()
        l_copy(peer_of(i), me, peer_of(i)).start()
        return carry

    each_chip(share)

    loads[2].wait()
    loads[3].wait()
    loads[4].wait()
    lane = lax.broadcasted_iota(jnp.int32, (1, group, LANES), 2)
    position = parity * keys + lax.broadcasted_iota(jnp.int32, (1, group, keys), 2)
    suf_bias = jnp.where(position < len_ref[row], 0.0, DEAD)
    token = lax.broadcasted_iota(jnp.int32, (2, group, 1), 0)
    visible = token >= parity
    q_copy(partner, partner, me).wait_recv()
    loads[5].wait()
    loads[6].wait()
    stat = jnp.zeros((2, group, LANES), jnp.float32)
    for pair in range(kvh // 2):
        q_pair = q_all[pl.ds(2 * row, 2), 2 * group * pair : 2 * group * (pair + 1), :].astype(jnp.float32)
        made = []
        for half in range(2):
            h = 2 * pair + half
            cols = slice(h * HD, (h + 1) * HD)
            q_head = q_pair[:, half * group : (half + 1) * group, :]
            scores = lax.dot_general(
                q_head.reshape(2 * group, HD).astype(jnp.bfloat16), sk[:, cols], NT,
                preferred_element_type=jnp.float32,
            ).reshape(2, group, keys)
            top, total, out = softmax_terms(scores, suf_bias, sv[:, cols])
            new_key = nk_ref[0:1, cols].astype(jnp.float32).reshape(1, 1, HD)
            new_value = nv_ref[0:1, cols].astype(jnp.float32).reshape(1, 1, HD)
            own = jnp.where(visible, jnp.sum(q_head * new_key, axis=-1, keepdims=True), DEAD)
            joint = jnp.maximum(top, own)
            old_scale = jnp.exp2((top - joint) * COEF)
            own_scale = jnp.exp2((own - joint) * COEF)
            total = old_scale * total + own_scale
            out = old_scale * out + own_scale * new_value
            made.append(out / jnp.maximum(total, 1.0))
            stat = jnp.where(lane == h, joint, stat)
            stat = jnp.where(lane == kvh + h, total, stat)
        suf_units[:, 2 * group * pair : 2 * group * (pair + 1), :] = jnp.concatenate(made, axis=1).astype(jnp.bfloat16)
    suf_stats[...] = stat
    in_units[chips] = suf_units[parity]
    in_stats[chips] = suf_stats[parity]
    suffix_copies = [
        pltpu.make_async_remote_copy(
            src_ref=source.at[1 - parity], dst_ref=target.at[chips + 1],
            send_sem=p_send.at[index], recv_sem=p_recv.at[index],
            device_id=(part, partner), device_id_type=MESH,
        )
        for index, (source, target) in enumerate(((suf_units, in_units), (suf_stats, in_stats)))
    ]
    for copy in suffix_copies:
        copy.start()

    l_copy(partner, partner, me).wait_recv()
    flip = 1 - 2 * parity

    def forward(i, carry):
        slot = peer_of(i)
        q_copy(partner, slot, slot + flip).wait_recv()
        q_copy(partner, slot, slot + flip).start()
        l_copy(partner, slot, slot + flip).wait_recv()
        l_copy(partner, slot, slot + flip).start()
        return carry

    each_chip(forward)

    def arrive(i, carry):
        q_copy(partner, peer_of(i) + flip, me).wait_recv()
        l_copy(partner, peer_of(i) + flip, me).wait_recv()
        return carry

    each_chip(arrive)
    loads[7].wait()
    loads[8].wait()
    chunk = min(n, TOKENS)

    def over_chunks(work):
        if n > chunk:
            def step(c, carry):
                work(c * chunk)
                return carry

            lax.fori_loop(0, n // chunk, step, 0)
        else:
            work(0)

    def mask(start):
        both = lists[pl.ds(start, chunk)].reshape(chunk // 2, 2, 1, width)
        both = jnp.maximum(both[:, 0], both[:, 1])
        for b in range(blocks):
            hit = jnp.max(jnp.where(both == me * blocks + b, 0.0, DEAD), axis=-1, keepdims=True)
            bias_ref[pl.ds(start // 2, chunk // 2), :, b * BLOCK : (b + 1) * BLOCK] = jnp.broadcast_to(hit, (chunk // 2, 8, BLOCK))

    def span(pair, start):
        rows = slice(2 * group * pair, 2 * group * (pair + 1))
        q_pair = q_all[pl.ds(start, chunk), rows, :].astype(jnp.float32)
        stat = jnp.zeros((chunk, group, LANES), jnp.float32)
        made = []
        for half in range(2):
            h = 2 * pair + half
            cols = slice(h * HD, (h + 1) * HD)
            q_head = q_pair[:, half * group : (half + 1) * group, :]
            scores = lax.dot_general(
                q_head.reshape(chunk * group, HD).astype(jnp.bfloat16), dk[:, cols], NT,
                preferred_element_type=jnp.float32,
            ).reshape(chunk, group, keys)
            bias = jnp.broadcast_to(
                bias_ref[pl.ds(start // 2, chunk // 2)][:, None], (chunk // 2, 2, group, keys)
            ).reshape(chunk, group, keys)
            top, total, out = softmax_terms(scores, bias, dv[:, cols])
            made.append(out * (1.0 / jnp.maximum(total, 1.0)))
            stat = jnp.where(lane == h, top, stat)
            stat = jnp.where(lane == kvh + h, total, stat)
        unit = jnp.concatenate(made, axis=1).astype(jnp.bfloat16).reshape(chunk // 2, 2, 2 * group, HD)
        stat = stat.reshape(chunk // 2, 2, group, LANES)
        for side in range(2):
            units[side, pl.ds(start // 2, chunk // 2), rows, :] = unit[:, side]
            stats[pair, side, pl.ds(start // 2, chunk // 2)] = stat[:, side]

    def aligned(values):
        return pltpu.roll(values.reshape(-1, LANES), LANES - kvh, 1).reshape(values.shape)

    def merge(pair):
        rows = slice(2 * group * pair, 2 * group * (pair + 1))
        mate_stats_copy(pair).wait()
        mate_copy(pair).wait()
        mine, other = stats[pair, parity], mate_stats[pair]
        joint = jnp.maximum(mine, other)
        mine_part = jnp.exp2((mine - joint) * COEF) * aligned(mine)
        other_part = jnp.exp2((other - joint) * COEF) * aligned(other)
        total = mine_part + other_part
        shares = 1.0 / jnp.maximum(total, 1.0)
        mine_part = mine_part * shares
        other_part = other_part * shares
        shifted = pltpu.roll(total.reshape(-1, LANES), kvh, 1).reshape(total.shape)
        fresh = jnp.where(lane < kvh, joint, shifted)
        fresh = jnp.where(lax.rem(lane, kvh) // 2 == pair, fresh, 0.0)
        merged_stats[...] = fresh if pair == 0 else merged_stats[...] + fresh
        first = units[parity, :, rows, :].astype(jnp.float32)
        second = mate_units[:, rows, :].astype(jnp.float32)
        made = []
        for half in range(2):
            h = 2 * pair + half
            part_rows = slice(half * group, (half + 1) * group)
            made.append(
                mine_part[:, :, h : h + 1] * first[:, part_rows, :]
                + other_part[:, :, h : h + 1] * second[:, part_rows, :]
            )
        merged[:, rows, :] = jnp.concatenate(made, axis=1).astype(jnp.bfloat16)

        def deliver_piece(i, carry):
            u_piece(peer_of(i), row, pair).start()
            return carry

        if pair % 2 == 1:
            each_chip(deliver_piece)

    over_chunks(mask)
    pairs_here = kvh // 2
    for pair in range(pairs_here):
        over_chunks(functools.partial(span, pair))
        mate_stats_copy(pair).start()
        mate_copy(pair).start()
        if pair > 0:
            merge(pair - 1)
    merge(pairs_here - 1)

    def deliver(i, carry):
        s_copy(peer_of(i), row).start()
        return carry

    each_chip(deliver)
    in_units[row] = merged[row]
    in_stats[row] = merged_stats[row]
    q_copy(partner, me, partner).wait_send()
    l_copy(partner, me, partner).wait_send()

    def q_sent(i, carry):
        q_copy(peer_of(i), me, peer_of(i)).wait_send()
        l_copy(peer_of(i), me, peer_of(i)).wait_send()
        q_copy(partner, peer_of(i), peer_of(i) + flip).wait_send()
        l_copy(partner, peer_of(i), peer_of(i) + flip).wait_send()
        return carry

    each_chip(q_sent)
    for copy in suffix_copies:
        copy.wait()

    def collect(i, carry):
        s_copy(peer_of(i), peer_of(i) // 2).wait_recv()
        u_copy(peer_of(i), peer_of(i) // 2).wait_recv()
        return carry

    each_chip(collect)

    tops = in_stats[...]
    ceiling = jnp.max(tops, axis=0, keepdims=True)
    spread = jnp.exp2((tops - ceiling) * COEF)
    weight = spread * aligned(tops)
    weight = weight / jnp.sum(weight, axis=0, keepdims=True)
    for pair in range(kvh // 2):
        parts = in_units[:, 2 * group * pair : 2 * group * (pair + 1), :].astype(jnp.float32)
        ends = []
        for half in range(2):
            h = 2 * pair + half
            ends.append(jnp.sum(weight[:, :, h : h + 1] * parts[:, half * group : (half + 1) * group, :], axis=0))
        out_ref[2 * group * pair : 2 * group * (pair + 1), :] = jnp.concatenate(ends, axis=0).astype(out_ref.dtype)

    def u_sent(i, carry):
        s_copy(peer_of(i), row).wait_send()
        u_copy(peer_of(i), row).wait_send()
        return carry

    each_chip(u_sent)


def per_device(n, queries, new_keys, new_values, doc_keys, doc_values, suffix_keys, suffix_values, keep_lists, suffix_lengths):
    heads = queries.shape[1] // HD
    kvh = new_keys.shape[1] // HD
    group = heads // kvh
    width = -(-2 * keep_lists.shape[1] // LANES) * LANES
    keys, columns = doc_keys.shape
    hbm = pl.BlockSpec(memory_space=pltpu.HBM)
    dma = pltpu.SemaphoreType.DMA
    out = pl.pallas_call(
        functools.partial(kernel, n, kvh, group),
        out_shape=jax.ShapeDtypeStruct((heads, HD), jnp.bfloat16),
        in_specs=[hbm] * 9,
        out_specs=pl.BlockSpec(memory_space=pltpu.VMEM),
        scratch_shapes=[
            pltpu.SMEM(suffix_lengths.shape, jnp.int32),
            pltpu.VMEM(queries.shape, jnp.bfloat16),
            pltpu.VMEM(new_keys.shape, jnp.bfloat16),
            pltpu.VMEM(new_values.shape, jnp.bfloat16),
            pltpu.VMEM(keep_lists.shape, jnp.int32),
            pltpu.VMEM((keys, columns), jnp.bfloat16),
            pltpu.VMEM((keys, columns), jnp.bfloat16),
            pltpu.VMEM(suffix_keys.shape, jnp.bfloat16),
            pltpu.VMEM(suffix_keys.shape, jnp.bfloat16),
            pltpu.VMEM((heads, HD), jnp.float32),
            pltpu.VMEM((n, heads, HD), jnp.bfloat16),
            pltpu.VMEM((n, 1, width), jnp.int32),
            pltpu.VMEM((n // 2, 8, keys), jnp.float32),
            pltpu.VMEM((2, n // 2, heads, HD), jnp.bfloat16),
            pltpu.VMEM((kvh // 2, 2, n // 2, group, LANES), jnp.float32),
            pltpu.VMEM((n // 2, heads, HD), jnp.bfloat16),
            pltpu.VMEM((kvh // 2, n // 2, group, LANES), jnp.float32),
            pltpu.VMEM((n // 2, heads, HD), jnp.bfloat16),
            pltpu.VMEM((n // 2, group, LANES), jnp.float32),
            pltpu.VMEM((2, heads, HD), jnp.bfloat16),
            pltpu.VMEM((2, group, LANES), jnp.float32),
            pltpu.VMEM((n // 2 + 2, heads, HD), jnp.bfloat16),
            pltpu.VMEM((n // 2 + 2, group, LANES), jnp.float32),
            dma((9,)),
            dma((n,)), dma((n,)), dma((n,)), dma((n,)),
            dma((kvh // 2,)), dma((kvh // 2,)), dma((kvh // 2,)), dma((kvh // 2,)),
            dma((n // 2,)), dma((n // 2,)), dma((n // 2,)), dma((n // 2,)),
            dma((2,)), dma((2,)),
        ],
        compiler_params=pltpu.CompilerParams(
            collective_id=0, has_side_effects=True, vmem_limit_bytes=65000 * 1024
        ),
    )(suffix_lengths, queries, new_keys, new_values, keep_lists, doc_keys, doc_values, suffix_keys, suffix_values)
    return out.reshape(1, heads * HD)


def solution(mesh):
    rows = P(("parts", "seq"), None)
    return jax.shard_map(
        functools.partial(per_device, mesh.shape["seq"]),
        mesh=mesh,
        in_specs=(rows,) * 8 + (P("parts"),),
        out_specs=rows,
        check_vma=False,
    )
```

```python
import functools
import math

import jax
import jax.numpy as jnp
from jax import lax
from jax.experimental import pallas as pl
from jax.experimental.pallas import tpu as pltpu
from jax.sharding import PartitionSpec as P

HD = 128
BLOCK = 128
LANES = 128
ID_ROWS = 16
TOKENS = 16

DEAD = -1e30
FLOOR = -1e29
MESH = pl.DeviceIdType.MESH
COEF = HD ** (-0.5) * math.log2(math.e)
NT = (((1,), (1,)), ((), ()))
NN = (((1,), (0,)), ((), ()))


def softmax_terms(scores, bias, values):
    rows, group, keys = scores.shape
    masked = scores + bias
    top = jnp.maximum(jnp.max(masked, axis=-1, keepdims=True), FLOOR)
    weights = jnp.exp2((masked - top) * COEF)
    total = jnp.sum(weights, axis=-1, keepdims=True)
    out = lax.dot_general(
        weights.reshape(rows * group, keys).astype(jnp.bfloat16),
        values,
        NN,
        preferred_element_type=jnp.float32,
    )
    return top, total, out.reshape(rows, group, HD)


def kernel(
    n, kvh, group,
    len_hbm, q_hbm, nk_hbm, nv_hbm, keep_hbm, dk_hbm, dv_hbm, sk_hbm, sv_hbm,
    out_ref,
    len_ref, q_ref, nk_ref, nv_ref, keep_ref,
    dk, dv, sk, sv, q_rows, q_all, bias_ref, units, stats, mate_units, mate_stats, merged, merged_stats, suf_units, suf_stats,
    in_units, in_stats,
    load_sem, q_send, q_recv, m_send, m_recv, u_send, u_recv, s_send, s_recv, p_send, p_recv,
):
    part = lax.axis_index("parts")
    me = lax.axis_index("seq")
    row = me // 2
    parity = me % 2
    partner = me + 1 - 2 * parity
    chips = n // 2
    heads = kvh * group
    keys = dk.shape[0]
    blocks = keys // BLOCK

    def peer_of(i):
        return lax.rem(me + 2 * i, n)

    barrier = pltpu.get_barrier_semaphore()
    pl.semaphore_signal(barrier, inc=1, device_id=(part, partner), device_id_type=MESH)

    def greet(i, carry):
        pl.semaphore_signal(barrier, inc=1, device_id=(part, peer_of(i)), device_id_type=MESH)
        return carry

    lax.fori_loop(1, chips, greet, 0)

    loads = []
    pairs = (
        (q_hbm, q_ref), (keep_hbm, keep_ref), (len_hbm, len_ref), (nk_hbm, nk_ref), (nv_hbm, nv_ref),
        (sk_hbm, sk), (sv_hbm, sv), (dk_hbm, dk), (dv_hbm, dv),
    )
    for index, (source, target) in enumerate(pairs):
        load = pltpu.make_async_copy(source, target, load_sem.at[index])
        load.start()
        loads.append(load)

    loads[0].wait()
    for h in range(heads):
        q_rows[h : h + 1, :] = q_ref[0:1, h * HD : (h + 1) * HD].astype(jnp.float32)
    kept = keep_ref.shape[1]
    width = -(-2 * kept // LANES) * LANES
    loads[1].wait()
    ids = keep_ref[...]
    blank = jnp.full((1, kept), -1, jnp.int32)
    pieces = [jnp.where(parity == 0, ids, blank), jnp.where(parity == 1, ids, blank)]
    if width > 2 * kept:
        pieces.append(jnp.full((1, width - 2 * kept), -1, jnp.int32))
    ids = jnp.concatenate(pieces, axis=1)
    q_rows[heads:, :] = jnp.zeros((ID_ROWS, LANES), jnp.float32)
    for w in range(width // LANES):
        piece = ids[:, w * LANES : (w + 1) * LANES]
        low = heads + w
        high = heads + ID_ROWS // 2 + w
        q_rows[low : low + 1, :] = (piece & 255).astype(jnp.float32)
        q_rows[high : high + 1, :] = (piece >> 8).astype(jnp.float32)
    q_all[me] = q_rows[...].astype(jnp.bfloat16)

    pl.semaphore_wait(barrier, chips)

    def q_copy(device, slot, send):
        return pltpu.make_async_remote_copy(
            src_ref=q_all.at[slot], dst_ref=q_all.at[slot],
            send_sem=q_send.at[send], recv_sem=q_recv.at[slot],
            device_id=(part, device), device_id_type=MESH,
        )

    def mate_copy(pair):
        rows = slice(2 * group * pair, 2 * group * (pair + 1))
        return pltpu.make_async_remote_copy(
            src_ref=units.at[1 - parity, :, rows, :], dst_ref=mate_units.at[:, rows, :],
            send_sem=m_send.at[pair], recv_sem=m_recv.at[pair],
            device_id=(part, partner), device_id_type=MESH,
        )

    def mate_stats_copy():
        return pltpu.make_async_remote_copy(
            src_ref=stats.at[1 - parity], dst_ref=mate_stats,
            send_sem=m_send.at[kvh // 2], recv_sem=m_recv.at[kvh // 2],
            device_id=(part, partner), device_id_type=MESH,
        )

    def u_copy(device, target):
        return pltpu.make_async_remote_copy(
            src_ref=merged.at[device // 2], dst_ref=in_units.at[target],
            send_sem=u_send.at[device // 2], recv_sem=u_recv.at[target],
            device_id=(part, device), device_id_type=MESH,
        )

    def s_copy(device, target):
        return pltpu.make_async_remote_copy(
            src_ref=merged_stats.at[device // 2], dst_ref=in_stats.at[target],
            send_sem=s_send.at[device // 2], recv_sem=s_recv.at[target],
            device_id=(part, device), device_id_type=MESH,
        )

    q_copy(partner, me, partner).start()

    def share(i, carry):
        q_copy(peer_of(i), me, peer_of(i)).start()
        return carry

    lax.fori_loop(1, chips, share, 0)

    loads[2].wait()
    loads[3].wait()
    loads[4].wait()
    lane = lax.broadcasted_iota(jnp.int32, (1, group, LANES), 2)
    position = parity * keys + lax.broadcasted_iota(jnp.int32, (1, group, keys), 2)
    suf_bias = jnp.where(position < len_ref[row], 0.0, DEAD)
    token = lax.broadcasted_iota(jnp.int32, (2, group, 1), 0)
    visible = token >= parity
    q_copy(partner, partner, me).wait_recv()
    loads[5].wait()
    loads[6].wait()
    stat = jnp.zeros((2, group, LANES), jnp.float32)
    for pair in range(kvh // 2):
        q_pair = q_all[pl.ds(2 * row, 2), 2 * group * pair : 2 * group * (pair + 1), :].astype(jnp.float32)
        made = []
        for half in range(2):
            h = 2 * pair + half
            cols = slice(h * HD, (h + 1) * HD)
            q_head = q_pair[:, half * group : (half + 1) * group, :]
            scores = lax.dot_general(
                q_head.reshape(2 * group, HD).astype(jnp.bfloat16), sk[:, cols], NT,
                preferred_element_type=jnp.float32,
            ).reshape(2, group, keys)
            top, total, out = softmax_terms(scores, suf_bias, sv[:, cols])
            new_key = nk_ref[0:1, cols].astype(jnp.float32).reshape(1, 1, HD)
            new_value = nv_ref[0:1, cols].astype(jnp.float32).reshape(1, 1, HD)
            own = jnp.where(visible, jnp.sum(q_head * new_key, axis=-1, keepdims=True), DEAD)
            joint = jnp.maximum(top, own)
            old_scale = jnp.exp2((top - joint) * COEF)
            own_scale = jnp.exp2((own - joint) * COEF)
            total = old_scale * total + own_scale
            out = old_scale * out + own_scale * new_value
            made.append(out / jnp.maximum(total, 1.0))
            stat = jnp.where(lane == h, joint, stat)
            stat = jnp.where(lane == kvh + h, total, stat)
        suf_units[:, 2 * group * pair : 2 * group * (pair + 1), :] = jnp.concatenate(made, axis=1).astype(jnp.bfloat16)
    suf_stats[...] = stat
    in_units[chips] = suf_units[parity]
    in_stats[chips] = suf_stats[parity]
    suffix_copies = [
        pltpu.make_async_remote_copy(
            src_ref=source.at[1 - parity], dst_ref=target.at[chips + 1],
            send_sem=p_send.at[index], recv_sem=p_recv.at[index],
            device_id=(part, partner), device_id_type=MESH,
        )
        for index, (source, target) in enumerate(((suf_units, in_units), (suf_stats, in_stats)))
    ]
    for copy in suffix_copies:
        copy.start()

    flip = 1 - 2 * parity

    def forward(i, carry):
        slot = peer_of(i)
        q_copy(partner, slot, slot + flip).wait_recv()
        q_copy(partner, slot, slot + flip).start()
        return carry

    lax.fori_loop(1, chips, forward, 0)

    def arrive(i, carry):
        q_copy(partner, peer_of(i) + flip, me).wait_recv()
        return carry

    lax.fori_loop(1, chips, arrive, 0)
    loads[7].wait()
    loads[8].wait()
    chunk = min(n, TOKENS)

    def span(start):
        tail = q_all[pl.ds(start, chunk), heads:, :].astype(jnp.float32)
        both = [
            tail[:, w : w + 1, :] + 256.0 * tail[:, ID_ROWS // 2 + w : ID_ROWS // 2 + w + 1, :]
            for w in range(width // LANES)
        ]
        both = jnp.concatenate(both, axis=-1).reshape(chunk // 2, 2, 1, width)
        both = jnp.maximum(both[:, 0], both[:, 1])
        for b in range(blocks):
            hit = jnp.max(jnp.where(both == (me * blocks + b).astype(jnp.float32), 0.0, DEAD), axis=-1, keepdims=True)
            bias_ref[:, :, b * BLOCK : (b + 1) * BLOCK] = jnp.broadcast_to(hit, (chunk // 2, 8, BLOCK))
        stat = jnp.zeros((chunk, group, LANES), jnp.float32)
        for pair in range(kvh // 2):
            q_pair = q_all[pl.ds(start, chunk), 2 * group * pair : 2 * group * (pair + 1), :].astype(jnp.float32)
            made = []
            for half in range(2):
                h = 2 * pair + half
                cols = slice(h * HD, (h + 1) * HD)
                q_head = q_pair[:, half * group : (half + 1) * group, :]
                scores = lax.dot_general(
                    q_head.reshape(chunk * group, HD).astype(jnp.bfloat16), dk[:, cols], NT,
                    preferred_element_type=jnp.float32,
                ).reshape(chunk, group, keys)
                bias = jnp.broadcast_to(
                    bias_ref[...][:, None], (chunk // 2, 2, group, keys)
                ).reshape(chunk, group, keys)
                top, total, out = softmax_terms(scores, bias, dv[:, cols])
                made.append(out * (1.0 / jnp.maximum(total, 1.0)))
                stat = jnp.where(lane == h, top, stat)
                stat = jnp.where(lane == kvh + h, total, stat)
            unit = jnp.concatenate(made, axis=1).astype(jnp.bfloat16).reshape(chunk // 2, 2, 2 * group, HD)
            for side in range(2):
                units[side, pl.ds(start // 2, chunk // 2), 2 * group * pair : 2 * group * (pair + 1), :] = unit[:, side]
            if n == chunk:
                mate_copy(pair).start()
        stat = stat.reshape(chunk // 2, 2, group, LANES)
        for side in range(2):
            stats[side, pl.ds(start // 2, chunk // 2)] = stat[:, side]

    if n > chunk:
        def step(c, carry):
            span(c * chunk)
            return carry

        lax.fori_loop(0, n // chunk, step, 0)
        for pair in range(kvh // 2):
            mate_copy(pair).start()
    else:
        span(0)

    mate_stats_copy().start()

    mate_stats_copy().wait()
    mine, other = stats[parity], mate_stats[...]

    def aligned(values):
        return pltpu.roll(values.reshape(-1, LANES), LANES - kvh, 1).reshape(values.shape)

    joint = jnp.maximum(mine, other)
    mine_part = jnp.exp2((mine - joint) * COEF) * aligned(mine)
    other_part = jnp.exp2((other - joint) * COEF) * aligned(other)
    total = mine_part + other_part
    shares = 1.0 / jnp.maximum(total, 1.0)
    mine_part = mine_part * shares
    other_part = other_part * shares
    shifted = pltpu.roll(total.reshape(-1, LANES), kvh, 1).reshape(total.shape)
    merged_stats[...] = jnp.where(lane < kvh, joint, shifted)
    for pair in range(kvh // 2):
        rows = slice(2 * group * pair, 2 * group * (pair + 1))
        mate_copy(pair).wait()
        first = units[parity, :, rows, :].astype(jnp.float32)
        second = mate_units[:, rows, :].astype(jnp.float32)
        made = []
        for half in range(2):
            h = 2 * pair + half
            part_rows = slice(half * group, (half + 1) * group)
            made.append(
                mine_part[:, :, h : h + 1] * first[:, part_rows, :]
                + other_part[:, :, h : h + 1] * second[:, part_rows, :]
            )
        merged[:, rows, :] = jnp.concatenate(made, axis=1).astype(jnp.bfloat16)

    def deliver(i, carry):
        s_copy(peer_of(i), row).start()
        u_copy(peer_of(i), row).start()
        return carry

    lax.fori_loop(1, chips, deliver, 0)
    in_units[row] = merged[row]
    in_stats[row] = merged_stats[row]
    q_copy(partner, me, partner).wait_send()

    def q_sent(i, carry):
        q_copy(peer_of(i), me, peer_of(i)).wait_send()
        q_copy(partner, peer_of(i), peer_of(i) + flip).wait_send()
        return carry

    lax.fori_loop(1, chips, q_sent, 0)
    for copy in suffix_copies:
        copy.wait()

    def collect(i, carry):
        s_copy(peer_of(i), peer_of(i) // 2).wait_recv()
        u_copy(peer_of(i), peer_of(i) // 2).wait_recv()
        return carry

    lax.fori_loop(1, chips, collect, 0)

    tops = in_stats[...]
    ceiling = jnp.max(tops, axis=0, keepdims=True)
    spread = jnp.exp2((tops - ceiling) * COEF)
    weight = spread * aligned(tops)
    weight = weight / jnp.sum(weight, axis=0, keepdims=True)
    for pair in range(kvh // 2):
        parts = in_units[:, 2 * group * pair : 2 * group * (pair + 1), :].astype(jnp.float32)
        ends = []
        for half in range(2):
            h = 2 * pair + half
            ends.append(jnp.sum(weight[:, :, h : h + 1] * parts[:, half * group : (half + 1) * group, :], axis=0))
        out_ref[2 * group * pair : 2 * group * (pair + 1), :] = jnp.concatenate(ends, axis=0).astype(out_ref.dtype)

    def u_sent(i, carry):
        s_copy(peer_of(i), row).wait_send()
        u_copy(peer_of(i), row).wait_send()
        return carry

    lax.fori_loop(1, chips, u_sent, 0)


def per_device(n, queries, new_keys, new_values, doc_keys, doc_values, suffix_keys, suffix_values, keep_lists, suffix_lengths):
    heads = queries.shape[1] // HD
    kvh = new_keys.shape[1] // HD
    group = heads // kvh
    keys, columns = doc_keys.shape
    hbm = pl.BlockSpec(memory_space=pltpu.HBM)
    dma = pltpu.SemaphoreType.DMA
    out = pl.pallas_call(
        functools.partial(kernel, n, kvh, group),
        out_shape=jax.ShapeDtypeStruct((heads, HD), jnp.bfloat16),
        in_specs=[hbm] * 9,
        out_specs=pl.BlockSpec(memory_space=pltpu.VMEM),
        scratch_shapes=[
            pltpu.SMEM(suffix_lengths.shape, jnp.int32),
            pltpu.VMEM(queries.shape, jnp.bfloat16),
            pltpu.VMEM(new_keys.shape, jnp.bfloat16),
            pltpu.VMEM(new_values.shape, jnp.bfloat16),
            pltpu.VMEM(keep_lists.shape, jnp.int32),
            pltpu.VMEM((keys, columns), jnp.bfloat16),
            pltpu.VMEM((keys, columns), jnp.bfloat16),
            pltpu.VMEM(suffix_keys.shape, jnp.bfloat16),
            pltpu.VMEM(suffix_keys.shape, jnp.bfloat16),
            pltpu.VMEM((heads + ID_ROWS, HD), jnp.float32),
            pltpu.VMEM((n, heads + ID_ROWS, HD), jnp.bfloat16),
            pltpu.VMEM((min(n, TOKENS) // 2, 8, keys), jnp.float32),
            pltpu.VMEM((2, n // 2, heads, HD), jnp.bfloat16),
            pltpu.VMEM((2, n // 2, group, LANES), jnp.float32),
            pltpu.VMEM((n // 2, heads, HD), jnp.bfloat16),
            pltpu.VMEM((n // 2, group, LANES), jnp.float32),
            pltpu.VMEM((n // 2, heads, HD), jnp.bfloat16),
            pltpu.VMEM((n // 2, group, LANES), jnp.float32),
            pltpu.VMEM((2, heads, HD), jnp.bfloat16),
            pltpu.VMEM((2, group, LANES), jnp.float32),
            pltpu.VMEM((n // 2 + 2, heads, HD), jnp.bfloat16),
            pltpu.VMEM((n // 2 + 2, group, LANES), jnp.float32),
            dma((9,)),
            dma((n,)), dma((n,)),
            dma((kvh // 2 + 1,)), dma((kvh // 2 + 1,)),
            dma((n // 2,)), dma((n // 2,)), dma((n // 2,)), dma((n // 2,)),
            dma((2,)), dma((2,)),
        ],
        compiler_params=pltpu.CompilerParams(
            collective_id=0, has_side_effects=True, vmem_limit_bytes=65000 * 1024
        ),
    )(suffix_lengths, queries, new_keys, new_values, keep_lists, doc_keys, doc_values, suffix_keys, suffix_values)
    return out.reshape(1, heads * HD)


def solution(mesh):
    rows = P(("parts", "seq"), None)
    return jax.shard_map(
        functools.partial(per_device, mesh.shape["seq"]),
        mesh=mesh,
        in_specs=(rows,) * 8 + (P("parts"),),
        out_specs=rows,
        check_vma=False,
    )
```
